256 devices in a mesh: crop: 16 (over y, x), proto: 16 (over z, core).
Axes of the slice: x: 4, y: 4, z: 8, core: 2. Of those that a mesh axis runs over, the one named last changes fastest.
Arguments:
- student_rows: bfloat16 [4096, 256], P(('crop', 'proto')), may hold values from -0.5 to 0.5
- teacher_rows: bfloat16 [4096, 256], P(('crop', 'proto')), may hold values from -0.5 to 0.5
- student_protos: bfloat16 [131072, 256], P(('proto', 'crop')), may hold values from -0.5 to 0.5
- teacher_protos: bfloat16 [131072, 256], P(('proto', 'crop')), may hold values from -0.5 to 0.5
Outputs:
- row_grad: float32 [4096, 256], P(('crop', 'proto'))
- proto_grad: float32 [131072, 256], P(('proto', 'crop'))
The draws below stay inside these ranges and needn't reach their ends.
All inputs are finite; a program needn't handle non-finite values.
Results may differ from the reference program's by a relative error of at most 0.0025.
The reference program's roundings to bfloat16 on the way (of `grad_logits`) count: a program that leaves them out, or rounds other values in their place, can miss the bound.
Values may be sent and summed in bfloat16 or wider, within the bound.
No kernel may reach another device: no remote copies, remote signals or barrier semaphores. Data moves between devices by JAX's collectives and lax.ppermute only.
A program may use at most 64 MiB of HBM per device.

```python
import math
import jax
import jax.numpy as jnp
from jax import lax

D = 256
SWEEPS = 3
PROTOS = 131072
CROPS = 4096
N_CROP = 16


def cluster_directions(key):
    return jax.random.normal(key, (N_CROP, D), jnp.float32)


def noise_field(key, count):
    return jax.random.normal(key, (count, D), jnp.float32)


def draw_teacher_rows(key, part):
    directions = cluster_directions(key)
    key = jax.random.fold_in(key, 11)
    noise = noise_field(key, CROPS)
    strength = 0.37
    group = jnp.arange(CROPS, dtype=jnp.int32) // (CROPS // N_CROP)
    chosen = jnp.take(directions, group, axis=0)
    values = 0.0625 * (noise + strength * chosen)
    return jnp.clip(values, -0.5, 0.5).astype(jnp.bfloat16)


def draw_teacher_protos(key, part):
    directions = cluster_directions(key)
    key = jax.random.fold_in(key, 23)
    first_key, second_key, noise_key = jax.random.split(key, 3)
    first = jax.random.randint(first_key, (PROTOS,), 0, N_CROP)
    second = jax.random.randint(second_key, (PROTOS,), 0, N_CROP)
    cluster = jnp.minimum(first, second).astype(jnp.int32)
    noise = noise_field(noise_key, PROTOS)
    strength = 0.37
    chosen = jnp.take(directions, cluster, axis=0)
    values = 0.0625 * (noise + strength * chosen)
    return jnp.clip(values, -0.5, 0.5).astype(jnp.bfloat16)


def block_scale(own_key, shape, cuts, least, largest):
    factor_of = 1.0
    for position, shards_of in cuts:
        heights = jax.random.uniform(jax.random.fold_in(jax.random.fold_in(own_key, 6), position), (shards_of,), jnp.float32, least / len(cuts), largest / len(cuts))
        factor_of = factor_of * jnp.repeat(jnp.exp(heights), shape[position] // shards_of).reshape((-1,) + (1,) * (len(shape) - 1 - position))
    return factor_of


def bell_draw(key, dims, deviation, bound, cuts=(), kind=jnp.bfloat16):
    result = deviation * jax.random.normal(key, dims, jnp.float32)
    if cuts:
        result = result * block_scale(key, dims, cuts, -0.22, 0.18)
    return jnp.clip(result, -bound, bound).astype(kind)


def setup_inputs(seed: int = 0) -> dict:
    seeds = jax.random.split(jax.random.key(seed), 5)
    return {
        "student_rows": bell_draw(seeds[0], (CROPS, D), 0.0625, 0.5, ((0, 256),)),
        "teacher_rows": draw_teacher_rows(jax.random.fold_in(seeds[4], 71), 0),
        "student_protos": bell_draw(seeds[2], (PROTOS, D), 0.0625, 0.5, ((0, 256),)),
        "teacher_protos": draw_teacher_protos(jax.random.fold_in(seeds[4], 71), 0),
    }


TEACHER_TEMP = 0.04
STUDENT_TEMP = 0.1
EPSILON = 1e-06
BLOCK_COLS = 1024
HIGHEST = lax.Precision.HIGHEST

def normalize(raw):
    values = raw.astype(jnp.float32)
    inverse = lax.rsqrt(lax.optimization_barrier(jnp.sum(values * values, axis=1, keepdims=True)) + EPSILON)
    return (values * inverse, inverse)

def rounded(values):
    return lax.optimization_barrier(values.astype(jnp.bfloat16)).astype(jnp.float32)

def reference(student_rows, teacher_rows, student_protos, teacher_protos):
    student_unit, student_inverse = normalize(student_rows)
    teacher_unit, unused_one = normalize(teacher_rows)
    proto_unit, proto_inverse = normalize(student_protos)
    target_unit, unused_two = normalize(teacher_protos)
    student_feat = rounded(student_unit)
    teacher_feat = rounded(teacher_unit)
    student_weight = rounded(proto_unit)
    teacher_weight = rounded(target_unit)
    width = math.gcd(PROTOS, BLOCK_COLS)
    count = PROTOS // width
    features = student_feat.shape[1]
    student_blocks = student_weight.reshape(count, width, features)
    teacher_blocks = teacher_weight.reshape(count, width, features)
    factor = PROTOS / 16.0

    def teacher_exp(weights):
        return jnp.exp(jnp.dot(teacher_feat, weights.T, precision=HIGHEST) / TEACHER_TEMP)

    def student_exp(weights):
        return jnp.exp(jnp.dot(student_feat, weights.T, precision=HIGHEST) / STUDENT_TEMP)
    row_scale = jnp.ones((CROPS,), jnp.float32)
    col_scale = jnp.ones((PROTOS,), jnp.float32)
    for sweep in range(SWEEPS):
        scales_now = row_scale
        col_mass = lax.map(lambda weights: lax.optimization_barrier(jnp.sum(teacher_exp(weights) * scales_now[:, None], axis=0)), teacher_blocks)
        col_scale = 1.0 / col_mass.reshape(PROTOS)

        def add_rows(total, pieces):
            return (total + lax.optimization_barrier(jnp.sum(teacher_exp(pieces[0]) * pieces[1][None, :], axis=1)), None)
        row_mass, unused_three = lax.scan(add_rows, jnp.zeros((CROPS,), jnp.float32), (teacher_blocks, col_scale.reshape(count, width)))
        row_scale = 1.0 / row_mass

    def add_student(total, weights):
        return (total + lax.optimization_barrier(jnp.sum(student_exp(weights), axis=1)), None)
    student_total, unused_four = lax.scan(add_student, jnp.zeros((CROPS,), jnp.float32), student_blocks)

    def backward(feat_grad, pieces):
        teacher_w, student_w, scales = pieces
        target = teacher_exp(teacher_w) * scales[None, :] * row_scale[:, None]
        prob = student_exp(student_w) / student_total[:, None]
        grad_logits = rounded((prob - target) * factor)
        feat_grad = feat_grad + jnp.dot(grad_logits, student_w, precision=HIGHEST)
        weight_grad = jnp.dot(grad_logits.T, student_feat, precision=HIGHEST)
        return (feat_grad, weight_grad)
    feat_grad, weight_blocks = lax.scan(backward, jnp.zeros((CROPS, features), jnp.float32), (teacher_blocks, student_blocks, col_scale.reshape(count, width)))
    weight_grad = weight_blocks.reshape(PROTOS, features)
    row_grad = (feat_grad - student_unit * lax.optimization_barrier(jnp.sum(student_unit * feat_grad, axis=1, keepdims=True))) * student_inverse
    proto_grad = (weight_grad - proto_unit * lax.optimization_barrier(jnp.sum(proto_unit * weight_grad, axis=1, keepdims=True))) * proto_inverse
    return (row_grad, proto_grad)
```

```python
import jax
import jax.numpy as jnp
from jax import lax
from jax.sharding import Mesh, PartitionSpec as P

SWEEPS = 3
TEACHER_TEMP = 0.04
STUDENT_TEMP = 0.1
EPSILON = 1e-06
ROWS = ("y", "z")


def normalize(raw):
    values = raw.astype(jnp.float32)
    inverse = lax.rsqrt(jnp.sum(values * values, axis=1, keepdims=True) + EPSILON)
    return (values * inverse, inverse)


def scores(rows, weights):
    return lax.dot_general(
        rows, weights, (((1,), (1,)), ((), ())), preferred_element_type=jnp.float32
    )


def shift(values, axis, step):
    size = lax.axis_size(axis)
    return lax.ppermute(values, axis, [(i, (i + step) % size) for i in range(size)])


def spread(values):
    count = lax.axis_size(ROWS)
    return lax.all_to_all(
        jnp.broadcast_to(values[None], (count,) + values.shape), ROWS, 0, 0, tiled=True
    )


def gather_rows(feat):
    own = spread(feat).reshape(-1, feat.shape[1])
    return jnp.concatenate([own, shift(own, "core", 1)], axis=0)


def gather_protos(weight):
    return jnp.concatenate([weight] + [shift(weight, "x", k) for k in (1, 2, 3)], axis=0)


def sum_columns(local):
    blocks = local.reshape(4, -1)
    total = blocks
    for k in (1, 2, 3):
        total = total + shift(jnp.roll(blocks, k, axis=0), "x", k)
    return total.reshape(-1)


def sum_rows(local):
    half = local.shape[0] // 2
    both = local + shift(jnp.concatenate([local[half:], local[:half]]), "core", 1)
    return jnp.sum(spread(both.reshape(-1, 128)), axis=0).reshape(-1)


def body(student_rows, teacher_rows, student_protos, teacher_protos):
    student_unit, student_inverse = normalize(student_rows)
    teacher_unit, unused_one = normalize(teacher_rows)
    proto_unit, proto_inverse = normalize(student_protos)
    target_unit, unused_two = normalize(teacher_protos)
    teacher_feat = gather_rows(teacher_unit.astype(jnp.bfloat16))
    teacher_weight = gather_protos(target_unit.astype(jnp.bfloat16))
    student_feat = gather_rows(student_unit.astype(jnp.bfloat16))
    student_weight = gather_protos(proto_unit.astype(jnp.bfloat16))
    own_rows = student_rows.shape[0]
    own_protos = student_protos.shape[0]
    features = student_rows.shape[1]
    factor = own_protos * 256 / 16.0

    teacher_exp = jnp.exp(scores(teacher_feat, teacher_weight) / TEACHER_TEMP)
    student_exp = jnp.exp(scores(student_feat, student_weight) / STUDENT_TEMP)
    student_total = sum_rows(jnp.sum(student_exp, axis=1))

    row_scale = jnp.ones((teacher_feat.shape[0],), jnp.float32)
    for sweep in range(SWEEPS):
        col_scale = 1.0 / sum_columns(jnp.sum(teacher_exp * row_scale[:, None], axis=0))
        row_scale = 1.0 / sum_rows(jnp.sum(teacher_exp * col_scale[None, :], axis=1))

    target = teacher_exp * col_scale[None, :] * row_scale[:, None]
    prob = student_exp / student_total[:, None]
    grad_logits = ((prob - target) * factor).astype(jnp.bfloat16)
    feat_grad = jnp.dot(grad_logits, student_weight, preferred_element_type=jnp.float32)
    weight_grad = lax.dot_general(
        grad_logits, student_feat, (((0,), (0,)), ((), ())), preferred_element_type=jnp.float32
    )
    half = feat_grad.shape[0] // 2
    feat_pair = feat_grad[:half] + shift(feat_grad[half:], "core", 1)
    feat_share = jnp.sum(
        lax.all_to_all(feat_pair.reshape(-1, own_rows, features), ROWS, 0, 0, tiled=True), axis=0
    )
    weight_parts = weight_grad.reshape(4, own_protos, features)
    weight_share = weight_parts[0]
    for k in (1, 2, 3):
        weight_share = weight_share + shift(weight_parts[k], "x", -k)
    row_grad = (
        feat_share - student_unit * jnp.sum(student_unit * feat_share, axis=1, keepdims=True)
    ) * student_inverse
    proto_grad = (
        weight_share - proto_unit * jnp.sum(proto_unit * weight_share, axis=1, keepdims=True)
    ) * proto_inverse
    return (row_grad, proto_grad)


def solution(mesh):
    fine = Mesh(mesh.devices.reshape(4, 4, 8, 2), ("y", "x", "z", "core"))
    rows = P(("y", "x", "z", "core"), None)
    protos = P(("z", "core", "y", "x"), None)
    return jax.shard_map(
        body,
        mesh=fine,
        in_specs=(rows, rows, protos, protos),
        out_specs=(rows, protos),
        check_vma=False,
    )
```

```python
import functools

import jax
import jax.numpy as jnp
from jax import lax
from jax.experimental import pallas as pl
from jax.experimental.pallas import tpu as pltpu
from jax.sharding import Mesh, PartitionSpec as P

SWEEPS = 3
TEACHER_TEMP = 0.04
STUDENT_TEMP = 0.1
EPSILON = 1e-06
ROWS = ("y", "z")
STEPS = 4
LANES = 128
TILE = 256

f32 = jnp.float32
bf16 = jnp.bfloat16
VMEM = pl.BlockSpec(memory_space=pltpu.VMEM)


def inverse_norm(values):
    return lax.rsqrt(jnp.sum(values * values, axis=1, keepdims=True) + EPSILON)


def unit(raw):
    values = raw.astype(f32)
    return (values * inverse_norm(values)).astype(bf16)


def call(kernel, outs, operands, flops, name):
    return pl.pallas_call(
        kernel,
        out_shape=outs,
        in_specs=[VMEM] * len(operands),
        out_specs=jax.tree.map(lambda unused: VMEM, outs),
        compiler_params=pltpu.CompilerParams(vmem_limit_bytes=16 * 2**20),
        cost_estimate=pl.CostEstimate(flops=flops, bytes_accessed=2**20, transcendentals=0),
        name=name,
    )(*operands)


def column(values):
    return jnp.broadcast_to(values, (LANES, LANES)).T


def row_of_sums(block):
    return jnp.sum(block.T, axis=0, keepdims=True)


def lane_sum(values):
    total = values[:, :LANES]
    for at in range(LANES, values.shape[1], LANES):
        total = total + values[:, at : at + LANES]
    return total


def store_rolled(outs, block, values):
    for step, out in enumerate(outs):
        at = (block + step) % STEPS
        out[at : at + 1, :] = values


def load_features(first, own, sib, protos, feat_ref, weight_ref):
    half, block, width = own.shape[0], protos[0].shape[0], protos[0].shape[1]
    feat_ref[:half, :] = unit(own[:, first : first + width])
    feat_ref[half:, :] = unit(sib[:, first : first + width])
    for k, proto in enumerate(protos):
        weight_ref[k * block : (k + 1) * block, :] = unit(proto[...])


def scores(rows, weights):
    return lax.dot_general(rows, weights, (((1,), (1,)), ((), ())), preferred_element_type=f32)


def teacher_kernel(own, sib, p0, p1, p2, p3, exp_ref, m0, m1, m2, m3, feat_ref, weight_ref):
    load_features(0, own, sib, (p0, p1, p2, p3), feat_ref, weight_ref)
    rows, block = feat_ref.shape[0], p0.shape[0]
    for k in range(STEPS):
        cols = slice(k * block, (k + 1) * block)
        total = jnp.zeros((8, block), f32)
        for at in range(0, rows, TILE):
            r = slice(at, at + TILE)
            part = jnp.exp(scores(feat_ref[r, :], weight_ref[cols, :]) * (1.0 / TEACHER_TEMP))
            exp_ref[r, cols] = part
            total = total + jnp.sum(part.reshape(TILE // 8, 8, block), axis=0)
        store_rolled((m0, m1, m2, m3), k, jnp.sum(total, axis=0, keepdims=True))


def student_kernel(own, sib, p0, p1, p2, p3, exp_ref, sum_ref, feat_ref, weight_ref):
    width, block = p0.shape[1], p0.shape[0]
    load_features(width, own, sib, (p0, p1, p2, p3), feat_ref, weight_ref)
    rows = feat_ref.shape[0]
    for at in range(0, rows, TILE):
        r = slice(at, at + TILE)
        total = jnp.zeros((TILE, LANES), f32)
        for k in range(STEPS):
            cols = slice(k * block, (k + 1) * block)
            part = jnp.exp(scores(feat_ref[r, :], weight_ref[cols, :]) * (1.0 / STUDENT_TEMP))
            exp_ref[r, cols] = part
            total = total + lane_sum(part)
        for t in range(TILE // LANES):
            i = at // LANES + t
            sum_ref[i : i + 1, :] = row_of_sums(total[t * LANES : (t + 1) * LANES])


def column_kernel(exp_ref, mass_ref, m0, m1, m2, m3):
    scale = 1.0 / jnp.sum(mass_ref[...], axis=0)
    rows, cols = exp_ref.shape
    block = cols // STEPS
    wide = 2 * block
    for h in range(cols // wide):
        total = jnp.zeros((8, wide), f32)
        for i in range(rows // LANES):
            col = column(scale[i : i + 1, :])
            for j in range(0, LANES, 8):
                at = i * LANES + j
                factor = jnp.concatenate([col[j : j + 8, :]] * (wide // LANES), axis=1)
                total = total + exp_ref[at : at + 8, h * wide : (h + 1) * wide] * factor
        whole = jnp.sum(total, axis=0, keepdims=True)
        for b in range(2):
            store_rolled((m0, m1, m2, m3), 2 * h + b, whole[:, b * block : (b + 1) * block])


def row_kernel(exp_ref, m0, m1, m2, m3, *refs):
    extra, (out_ref, swap_ref, scale_ref) = refs[:-3], refs[-3:]
    scale = 1.0 / (m0[...] + m1[...] + m2[...] + m3[...])
    scale_ref[...] = scale
    rows, cols = exp_ref.shape
    block = cols // STEPS
    count = rows // LANES
    for i in range(count):
        total = jnp.zeros((LANES, LANES), f32)
        for at in range(0, cols, LANES):
            k, o = at // block, at % block
            r = slice(i * LANES, (i + 1) * LANES)
            total = total + exp_ref[r, at : at + LANES] * scale[k : k + 1, o : o + LANES]
        out_ref[i : i + 1, :] = row_of_sums(total)
    for ref in extra:
        out_ref[count : 2 * count, :] = ref[...]
    for at in range(0, out_ref.shape[0], count):
        swap_ref[at : at + count // 2, :] = out_ref[at + count // 2 : at + count, :]
        swap_ref[at + count // 2 : at + count, :] = out_ref[at : at + count // 2, :]


def logits_kernel(factor, exp_t, exp_s, scale_ref, mass_ref, weight_ref, grad_ref, feat_ref):
    inverse = factor / jnp.sum(mass_ref[...], axis=0)
    rows, cols = exp_t.shape
    count, block = rows // LANES, cols // STEPS
    for i in range(count):
        r = slice(i * LANES, (i + 1) * LANES)
        row = column(inverse[i : i + 1, :])
        total = column(inverse[count + i : count + i + 1, :])
        for at in range(0, cols, LANES):
            k, o = at // block, at % block
            c = slice(at, at + LANES)
            target = exp_t[r, c] * scale_ref[k : k + 1, o : o + LANES] * row
            grad_ref[r, c] = (exp_s[r, c] * total - target).astype(bf16)
    feat_ref[...] = jnp.dot(grad_ref[...], weight_ref[...], preferred_element_type=f32)


def weight_kernel(grad_ref, feat_ref, *outs):
    block = outs[0].shape[0]
    for k, out in enumerate(outs):
        out[...] = lax.dot_general(
            grad_ref[:, k * block : (k + 1) * block],
            feat_ref[...],
            (((0,), (0,)), ((), ())),
            preferred_element_type=f32,
        )


def project(raw, grads):
    values = raw.astype(f32)
    inverse = inverse_norm(values)
    unit_rows = values * inverse
    return (grads - unit_rows * jnp.sum(unit_rows * grads, axis=1, keepdims=True)) * inverse


def row_grad_kernel(raw, parts, out):
    out[...] = project(raw[...], jnp.sum(parts[...], axis=0))


def proto_grad_kernel(raw, w0, w1, w2, w3, out):
    out[...] = project(raw[...], w0[...] + w1[...] + w2[...] + w3[...])


def shift(values, axis, step):
    size = lax.axis_size(axis)
    return lax.ppermute(values, axis, [(i, (i + step) % size) for i in range(size)])


def spread(values):
    count = lax.axis_size(ROWS)
    return lax.all_to_all(
        jnp.broadcast_to(values[None], (count,) + values.shape), ROWS, 0, 0, tiled=True
    )


def gather_protos(raw):
    return [raw] + [shift(raw, "x", k) for k in range(1, STEPS)]


def share(blocks):
    return [blocks[0]] + [shift(blocks[k], "x", k) for k in range(1, STEPS)]


def share_rows(mine, swapped):
    return spread(mine + shift(swapped, "core", 1))


def body(student_rows, teacher_rows, student_protos, teacher_protos):
    own_rows, width = student_rows.shape
    own_protos = student_protos.shape[0]
    rows = own_rows * lax.axis_size(ROWS) * lax.axis_size("core")
    cols = own_protos * STEPS
    factor = own_protos * 256 / 16.0
    work = 2 * rows * cols * width

    exps = pltpu.VMEM((rows, cols), f32)
    masses = [jax.ShapeDtypeStruct((STEPS, own_protos), f32)] * STEPS
    sums = jax.ShapeDtypeStruct((rows // LANES, LANES), f32)
    feats = pltpu.VMEM((rows, width), bf16)
    weights = pltpu.VMEM((cols, width), bf16)

    teacher_blocks = gather_protos(teacher_protos)
    student_blocks = gather_protos(student_protos)
    own = spread(jnp.concatenate([teacher_rows, student_rows], axis=1)).reshape(-1, 2 * width)
    sib = shift(own, "core", 1)

    exp_t, *mass = call(
        teacher_kernel, [exps] + masses + [feats, weights], (own, sib, *teacher_blocks), work, "teacher"
    )
    mass = mass[:STEPS]
    exp_s, student_sums, student_feat, student_weight = call(
        student_kernel, [exps, sums, feats, weights], (own, sib, *student_blocks), work, "student"
    )
    for sweep in range(SWEEPS):
        last = sweep + 1 == SWEEPS
        extra = (student_sums,) if last else ()
        out = jax.ShapeDtypeStruct((rows // LANES * (1 + len(extra)), LANES), f32)
        mine, swapped, scale = call(
            row_kernel, [out, out, masses[0]], (exp_t, *share(mass), *extra), work // 8, "rows"
        )
        row_masses = share_rows(mine, swapped)
        if not last:
            mass = call(column_kernel, masses, (exp_t, row_masses), work // 8, "columns")

    grads, feat_grad = call(
        functools.partial(logits_kernel, factor),
        [pltpu.VMEM((rows, cols), bf16), jax.ShapeDtypeStruct((rows, width), f32)],
        (exp_t, exp_s, scale, row_masses, student_weight),
        work,
        "logits",
    )
    weight_parts = call(
        weight_kernel,
        [jax.ShapeDtypeStruct((own_protos, width), f32)] * STEPS,
        (grads, student_feat),
        work,
        "weights",
    )
    half = rows // 2
    feat_pair = feat_grad[:half] + shift(feat_grad[half:], "core", 1)
    feat_share = lax.all_to_all(feat_pair.reshape(-1, own_rows, width), ROWS, 0, 0, tiled=True)
    weight_share = [weight_parts[0]] + [shift(weight_parts[k], "x", -k) for k in range(1, STEPS)]
    row_grad = call(
        row_grad_kernel,
        jax.ShapeDtypeStruct((own_rows, width), f32),
        (student_rows, feat_share),
        rows * width,
        "row_grad",
    )
    proto_grad = call(
        proto_grad_kernel,
        jax.ShapeDtypeStruct((own_protos, width), f32),
        (student_protos, *weight_share),
        own_protos * width,
        "proto_grad",
    )
    return (row_grad, proto_grad)


def solution(mesh):
    fine = Mesh(mesh.devices.reshape(4, 4, 8, 2), ("y", "x", "z", "core"))
    rows = P(("y", "x", "z", "core"), None)
    protos = P(("z", "core", "y", "x"), None)
    return jax.shard_map(
        body,
        mesh=fine,
        in_specs=(rows, rows, protos, protos),
        out_specs=(rows, protos),
        check_vma=False,
    )
```

```python
import functools

import jax
import jax.numpy as jnp
from jax import lax
from jax.experimental import pallas as pl
from jax.experimental.pallas import tpu as pltpu
from jax.sharding import Mesh, PartitionSpec as P

SWEEPS = 3
TEACHER_TEMP = 0.04
STUDENT_TEMP = 0.1
EPSILON = 1e-06
ROWS = ("y", "z")
STEPS = 4
LANES = 128
TILE = 256

f32 = jnp.float32
bf16 = jnp.bfloat16
VMEM = pl.BlockSpec(memory_space=pltpu.VMEM)


def inverse_norm(values):
    return lax.rsqrt(jnp.sum(values * values, axis=1, keepdims=True) + EPSILON)


def unit(raw):
    values = raw.astype(f32)
    return (values * inverse_norm(values)).astype(bf16)


def call(kernel, outs, operands, flops, name, scratch=(), after=(), where=VMEM):
    count = len(after)
    return pl.pallas_call(
        lambda *refs: kernel(*refs[count:]),
        out_shape=outs,
        in_specs=[pl.BlockSpec(memory_space=pl.ANY)] * count + [where] * len(operands),
        out_specs=jax.tree.map(lambda unused: VMEM, outs),
        scratch_shapes=scratch,
        compiler_params=pltpu.CompilerParams(vmem_limit_bytes=8 * 2**20),
        cost_estimate=pl.CostEstimate(flops=flops, bytes_accessed=2**20, transcendentals=0),
        name=name,
    )(*after, *operands)


def column(values):
    return jnp.broadcast_to(values, (LANES, LANES)).T


def row_of_sums(block):
    return jnp.sum(block.T, axis=0, keepdims=True)


def lane_sum(values):
    total = values[:, :LANES]
    for at in range(LANES, values.shape[1], LANES):
        total = total + values[:, at : at + LANES]
    return total


def store_rolled(outs, block, values):
    for step, out in enumerate(outs):
        at = (block + step) % STEPS
        out[at : at + 1, :] = values


def pack_kernel(first, second, out, held, arrived):
    copies = [
        pltpu.make_async_copy(ref, held.at[k], arrived.at[k]) for k, ref in enumerate((first, second))
    ]
    for copy in copies:
        copy.start()
    for copy in copies:
        copy.wait()
    packed = jnp.concatenate([held[0], held[1]], axis=1)
    for peer in range(out.shape[0]):
        out[peer] = packed


def unit_kernel(*refs):
    out, block = refs[-1], refs[0].shape[0]
    for k, ref in enumerate(refs[:-1]):
        out[k * block : (k + 1) * block, :] = unit(ref[...])


def load_features(first, own, sib, feat_ref):
    half, width = own.shape[0], feat_ref.shape[1]
    feat_ref[:half, :] = unit(own[:, first : first + width])
    feat_ref[half:, :] = unit(sib[:, first : first + width])


def scores(rows, weights):
    return lax.dot_general(rows, weights, (((1,), (1,)), ((), ())), preferred_element_type=f32)


def teacher_kernel(own, sib, weight_ref, exp_ref, m0, m1, m2, m3, feat_ref):
    load_features(0, own, sib, feat_ref)
    rows, block = feat_ref.shape[0], weight_ref.shape[0] // STEPS
    for k in range(STEPS):
        cols = slice(k * block, (k + 1) * block)
        total = jnp.zeros((8, block), f32)
        for at in range(0, rows, TILE):
            r = slice(at, at + TILE)
            part = jnp.exp(scores(feat_ref[r, :], weight_ref[cols, :]) * (1.0 / TEACHER_TEMP))
            exp_ref[r, cols] = part
            total = total + jnp.sum(part.reshape(TILE // 8, 8, block), axis=0)
        store_rolled((m0, m1, m2, m3), k, jnp.sum(total, axis=0, keepdims=True))


def student_kernel(own, sib, weight_ref, exp_ref, sum_ref, feat_ref):
    load_features(feat_ref.shape[1], own, sib, feat_ref)
    rows, block = feat_ref.shape[0], weight_ref.shape[0] // STEPS
    for at in range(0, rows, TILE):
        r = slice(at, at + TILE)
        total = jnp.zeros((TILE, LANES), f32)
        for k in range(STEPS):
            cols = slice(k * block, (k + 1) * block)
            part = jnp.exp(scores(feat_ref[r, :], weight_ref[cols, :]) * (1.0 / STUDENT_TEMP))
            exp_ref[r, cols] = part
            total = total + lane_sum(part)
        for t in range(TILE // LANES):
            i = at // LANES + t
            sum_ref[i : i + 1, :] = row_of_sums(total[t * LANES : (t + 1) * LANES])


def column_kernel(exp_ref, mass_ref, m0, m1, m2, m3):
    scale = 1.0 / jnp.sum(mass_ref[...], axis=0)
    rows, cols = exp_ref.shape
    block = cols // STEPS
    wide = 2 * block
    for h in range(cols // wide):
        total = jnp.zeros((8, wide), f32)
        for i in range(rows // LANES):
            col = column(scale[i : i + 1, :])
            for j in range(0, LANES, 8):
                at = i * LANES + j
                factor = jnp.concatenate([col[j : j + 8, :]] * (wide // LANES), axis=1)
                total = total + exp_ref[at : at + 8, h * wide : (h + 1) * wide] * factor
        whole = jnp.sum(total, axis=0, keepdims=True)
        for b in range(2):
            store_rolled((m0, m1, m2, m3), 2 * h + b, whole[:, b * block : (b + 1) * block])


def row_kernel(exp_ref, m0, m1, m2, m3, *refs):
    extra, (out_ref, swap_ref, scale_ref) = refs[:-3], refs[-3:]
    scale = 1.0 / (m0[...] + m1[...] + m2[...] + m3[...])
    scale_ref[...] = scale
    rows, cols = exp_ref.shape
    block = cols // STEPS
    count = rows // LANES
    for i in range(count):
        total = jnp.zeros((LANES, LANES), f32)
        for at in range(0, cols, LANES):
            k, o = at // block, at % block
            r = slice(i * LANES, (i + 1) * LANES)
            total = total + exp_ref[r, at : at + LANES] * scale[k : k + 1, o : o + LANES]
        out_ref[i : i + 1, :] = row_of_sums(total)
    for ref in extra:
        out_ref[count : 2 * count, :] = ref[...]
    for at in range(0, out_ref.shape[0], count):
        swap_ref[at : at + count // 2, :] = out_ref[at + count // 2 : at + count, :]
        swap_ref[at + count // 2 : at + count, :] = out_ref[at : at + count // 2, :]


def grads_kernel(
    factor, exp_t, exp_s, scale_ref, mass_ref, feat_ref, weight_ref, feat_out, w0, w1, w2a, w2b, w3, grad_ref
):
    inverse = factor / jnp.sum(mass_ref[...], axis=0)
    rows, cols = exp_t.shape
    count, block = rows // LANES, cols // STEPS
    row = [column(inverse[i : i + 1, :]) for i in range(count)]
    total = [column(inverse[count + i : count + i + 1, :]) for i in range(count)]
    for k, outs in enumerate(((w0,), (w1,), (w2a, w2b), (w3,))):
        for i in range(count):
            r = slice(i * LANES, (i + 1) * LANES)
            for o in range(0, block, LANES):
                c = slice(k * block + o, k * block + o + LANES)
                target = exp_t[r, c] * scale_ref[k : k + 1, o : o + LANES] * row[i]
                grad_ref[r, c] = (exp_s[r, c] * total[i] - target).astype(bf16)
        at = k * block
        for out in outs:
            size = out.shape[0]
            out[...] = lax.dot_general(
                grad_ref[:, at : at + size],
                feat_ref[...],
                (((0,), (0,)), ((), ())),
                preferred_element_type=f32,
            )
            at += size
    feat_out[...] = jnp.dot(grad_ref[...], weight_ref[...], preferred_element_type=f32)


def pair_kernel(mine, other, out):
    half = other.shape[0]
    out[...] = (mine[:half, :] + other[...]).reshape(out.shape)


def relay_kernel(forward, back, upper, lower, forward_out, back_out):
    half = upper.shape[0]
    forward_out[:half, :] = forward[:half, :] + upper[...]
    forward_out[half:, :] = forward[half:, :]
    back_out[:half, :] = back[:half, :]
    back_out[half:, :] = back[half:, :] + lower[...]


def project(raw, grads):
    values = raw.astype(f32)
    inverse = inverse_norm(values)
    unit_rows = values * inverse
    return (grads - unit_rows * jnp.sum(unit_rows * grads, axis=1, keepdims=True)) * inverse


def row_grad_kernel(raw, parts, out):
    out[...] = project(raw[...], jnp.sum(parts[...], axis=0))


def proto_grad_kernel(raw, mine, before, after, out):
    out[...] = project(raw[...], mine[...] + before[...] + after[...])


def shift(values, axis, step):
    size = lax.axis_size(axis)
    return lax.ppermute(values, axis, [(i, (i + step) % size) for i in range(size)])


def spread(values):
    count = lax.axis_size(ROWS)
    return lax.all_to_all(
        jnp.broadcast_to(values[None], (count,) + values.shape), ROWS, 0, 0, tiled=True
    )


def gather_protos(raw):
    return [raw] + [shift(raw, "x", k) for k in range(1, STEPS)]


def share(blocks):
    return [blocks[0]] + [shift(blocks[k], "x", k) for k in range(1, STEPS)]


def share_rows(mine, swapped):
    return spread(mine + shift(swapped, "core", 1))


def body(student_rows, teacher_rows, student_protos, teacher_protos):
    own_rows, width = student_rows.shape
    own_protos = student_protos.shape[0]
    rows = own_rows * lax.axis_size(ROWS) * lax.axis_size("core")
    cols = own_protos * STEPS
    factor = own_protos * 256 / 16.0
    work = 2 * rows * cols * width

    exps = pltpu.VMEM((rows, cols), f32)
    masses = [jax.ShapeDtypeStruct((STEPS, own_protos), f32)] * STEPS
    sums = jax.ShapeDtypeStruct((rows // LANES, LANES), f32)
    feats = pltpu.VMEM((rows, width), bf16)
    weights = pltpu.VMEM((cols, width), bf16)

    peers = lax.axis_size(ROWS)
    packed = call(
        pack_kernel,
        jax.ShapeDtypeStruct((peers, own_rows, 2 * width), bf16),
        (teacher_rows, student_rows),
        0,
        "pack",
        [pltpu.VMEM((2, own_rows, width), bf16), pltpu.SemaphoreType.DMA((2,))],
        where=pl.BlockSpec(memory_space=pltpu.HBM),
    )
    own = lax.all_to_all(packed, ROWS, 0, 0, tiled=True).reshape(-1, 2 * width)
    teacher_blocks = gather_protos(teacher_protos)
    teacher_weight = call(unit_kernel, weights, teacher_blocks, 100 * work, "teacher_units")
    student_protos, teacher_blocks[1] = lax.optimization_barrier((student_protos, teacher_blocks[1]))
    student_weight = call(unit_kernel, weights, gather_protos(student_protos), 0, "student_units")
    own, teacher_weight, student_weight = lax.optimization_barrier(
        (own, teacher_weight, student_weight)
    )
    sib = shift(own, "core", 1)

    exp_t, *mass = call(
        teacher_kernel, [exps] + masses + [feats], (own, sib, teacher_weight), work, "teacher"
    )
    mass = share(mass[:STEPS])
    exp_s, student_sums, student_feat = call(
        student_kernel, [exps, sums, feats], (own, sib, student_weight), work, "student"
    )
    for sweep in range(SWEEPS):
        last = sweep + 1 == SWEEPS
        extra = (student_sums,) if last else ()
        out = jax.ShapeDtypeStruct((rows // LANES * (1 + len(extra)), LANES), f32)
        mine, swapped, scale = call(
            row_kernel,
            [out, out, masses[0]],
            (exp_t, *mass, *extra),
            work // 8,
            "rows",
        )
        row_masses = share_rows(mine, swapped)
        if not last:
            mass = share(call(column_kernel, masses, (exp_t, row_masses), work // 8, "columns"))

    feat_grad, *weight_parts = call(
        functools.partial(grads_kernel, factor),
        [
            jax.ShapeDtypeStruct((size, width), f32)
            for size in (rows, own_protos, own_protos, own_protos // 2, own_protos // 2, own_protos)
        ],
        (exp_t, exp_s, scale, row_masses, student_feat, student_weight),
        2 * work,
        "grads",
        [pltpu.VMEM((rows, cols), bf16)],
    )
    half = rows // 2
    feat_pair = call(
        pair_kernel,
        jax.ShapeDtypeStruct((half // own_rows, own_rows, width), f32),
        (feat_grad, shift(feat_grad[half:], "core", 1)),
        100 * work,
        "pair",
    )
    feat_share = lax.all_to_all(feat_pair, ROWS, 0, 0, tiled=True)
    own_part, back_part, upper_part, lower_part, forward_part = weight_parts
    forward_part, back_part = call(
        relay_kernel,
        [jax.ShapeDtypeStruct((own_protos, width), f32)] * 2,
        (forward_part, back_part, shift(upper_part, "x", 1), shift(lower_part, "x", -1)),
        100 * work,
        "relay",
    )
    proto_grad = call(
        proto_grad_kernel,
        jax.ShapeDtypeStruct((own_protos, width), f32),
        (student_protos, own_part, shift(forward_part, "x", 1), shift(back_part, "x", -1)),
        0,
        "proto_grad",
    )
    row_grad = call(
        row_grad_kernel,
        jax.ShapeDtypeStruct((own_rows, width), f32),
        (student_rows, feat_share),
        0,
        "row_grad",
    )
    return (row_grad, proto_grad)


def solution(mesh):
    fine = Mesh(mesh.devices.reshape(4, 4, 8, 2), ("y", "x", "z", "core"))
    rows = P(("y", "x", "z", "core"), None)
    protos = P(("z", "core", "y", "x"), None)
    return jax.shard_map(
        body,
        mesh=fine,
        in_specs=(rows, rows, protos, protos),
        out_specs=(rows, protos),
        check_vma=False,
    )
```

```python
import functools

import jax
import jax.numpy as jnp
from jax import lax
from jax.experimental import pallas as pl
from jax.experimental.pallas import tpu as pltpu
from jax.sharding import Mesh, PartitionSpec as P

SWEEPS = 3
TEACHER_TEMP = 0.04
STUDENT_TEMP = 0.1
EPSILON = 1e-06
ROWS = ("y", "z")
STEPS = 4
LANES = 128
TILE = 256

f32 = jnp.float32
bf16 = jnp.bfloat16
VMEM = pl.BlockSpec(memory_space=pltpu.VMEM)


def inverse_norm(values):
    return lax.rsqrt(jnp.sum(values * values, axis=1, keepdims=True) + EPSILON)


def unit(raw):
    values = raw.astype(f32)
    return (values * inverse_norm(values)).astype(bf16)


def call(kernel, outs, operands, flops, name, scratch=(), after=(), where=VMEM):
    count = len(after)
    return pl.pallas_call(
        lambda *refs: kernel(*refs[count:]),
        out_shape=outs,
        in_specs=[pl.BlockSpec(memory_space=pl.ANY)] * count + [where] * len(operands),
        out_specs=jax.tree.map(lambda unused: VMEM, outs),
        scratch_shapes=scratch,
        compiler_params=pltpu.CompilerParams(vmem_limit_bytes=8 * 2**20),
        cost_estimate=pl.CostEstimate(flops=flops, bytes_accessed=2**20, transcendentals=0),
        name=name,
    )(*after, *operands)


def column(values):
    return jnp.broadcast_to(values, (LANES, LANES)).T


def row_of_sums(block):
    return jnp.sum(block.T, axis=0, keepdims=True)


def lane_sum(values):
    total = values[:, :LANES]
    for at in range(LANES, values.shape[1], LANES):
        total = total + values[:, at : at + LANES]
    return total


def store_rolled(outs, block, values):
    for step, out in enumerate(outs):
        at = (block + step) % STEPS
        out[at : at + 1, :] = values


def pack_kernel(first, second, out, held, arrived):
    copies = [
        pltpu.make_async_copy(ref, held.at[k], arrived.at[k]) for k, ref in enumerate((first, second))
    ]
    for copy in copies:
        copy.start()
    for copy in copies:
        copy.wait()
    packed = jnp.concatenate([held[0], held[1]], axis=1)
    for peer in range(out.shape[0]):
        out[peer] = packed


def halves_kernel(before, after, upper, lower):
    half = upper.shape[0]
    upper[...] = before[:half, :]
    lower[...] = after[half:, :]


def unit_kernel(*refs):
    out, at = refs[-1], 0
    for ref in refs[:-1]:
        out[at : at + ref.shape[0], :] = unit(ref[...])
        at += ref.shape[0]


def load_features(first, own, sib, feat_ref):
    half, width = own.shape[0], feat_ref.shape[1]
    feat_ref[:half, :] = unit(own[:, first : first + width])
    feat_ref[half:, :] = unit(sib[:, first : first + width])


def scores(rows, weights):
    return lax.dot_general(rows, weights, (((1,), (1,)), ((), ())), preferred_element_type=f32)


def teacher_kernel(own, sib, weight_ref, exp_ref, m0, m1, m2, m3, feat_ref):
    load_features(0, own, sib, feat_ref)
    rows, block = feat_ref.shape[0], weight_ref.shape[0] // STEPS
    for k in range(STEPS):
        cols = slice(k * block, (k + 1) * block)
        total = jnp.zeros((8, block), f32)
        for at in range(0, rows, TILE):
            r = slice(at, at + TILE)
            part = jnp.exp(scores(feat_ref[r, :], weight_ref[cols, :]) * (1.0 / TEACHER_TEMP))
            exp_ref[r, cols] = part
            total = total + jnp.sum(part.reshape(TILE // 8, 8, block), axis=0)
        store_rolled((m0, m1, m2, m3), k, jnp.sum(total, axis=0, keepdims=True))


def student_kernel(own, sib, weight_ref, exp_ref, sum_ref, feat_ref):
    load_features(feat_ref.shape[1], own, sib, feat_ref)
    rows, block = feat_ref.shape[0], weight_ref.shape[0] // STEPS
    for at in range(0, rows, TILE):
        r = slice(at, at + TILE)
        total = jnp.zeros((TILE, LANES), f32)
        for k in range(STEPS):
            cols = slice(k * block, (k + 1) * block)
            part = jnp.exp(scores(feat_ref[r, :], weight_ref[cols, :]) * (1.0 / STUDENT_TEMP))
            exp_ref[r, cols] = part
            total = total + lane_sum(part)
        for t in range(TILE // LANES):
            i = at // LANES + t
            sum_ref[i : i + 1, :] = row_of_sums(total[t * LANES : (t + 1) * LANES])


def column_kernel(exp_ref, mass_ref, m0, m1, m2, m3):
    scale = 1.0 / jnp.sum(mass_ref[...], axis=0)
    rows, cols = exp_ref.shape
    block = cols // STEPS
    wide = 2 * block
    for h in range(cols // wide):
        total = jnp.zeros((8, wide), f32)
        for i in range(rows // LANES):
            col = column(scale[i : i + 1, :])
            for j in range(0, LANES, 8):
                at = i * LANES + j
                factor = jnp.concatenate([col[j : j + 8, :]] * (wide // LANES), axis=1)
                total = total + exp_ref[at : at + 8, h * wide : (h + 1) * wide] * factor
        whole = jnp.sum(total, axis=0, keepdims=True)
        for b in range(2):
            store_rolled((m0, m1, m2, m3), 2 * h + b, whole[:, b * block : (b + 1) * block])


def row_kernel(exp_ref, m0, m1, m2, m3, *refs):
    extra, (out_ref, swap_ref, scale_ref) = refs[:-3], refs[-3:]
    scale = 1.0 / (m0[...] + m1[...] + m2[...] + m3[...])
    scale_ref[...] = scale
    rows, cols = exp_ref.shape
    block = cols // STEPS
    count = rows // LANES
    for i in range(count):
        total = jnp.zeros((LANES, LANES), f32)
        for at in range(0, cols, LANES):
            k, o = at // block, at % block
            r = slice(i * LANES, (i + 1) * LANES)
            total = total + exp_ref[r, at : at + LANES] * scale[k : k + 1, o : o + LANES]
        out_ref[i : i + 1, :] = row_of_sums(total)
    for ref in extra:
        out_ref[count : 2 * count, :] = ref[...]
    for at in range(0, out_ref.shape[0], count):
        swap_ref[at : at + count // 2, :] = out_ref[at + count // 2 : at + count, :]
        swap_ref[at + count // 2 : at + count, :] = out_ref[at : at + count // 2, :]


def grads_kernel(
    factor, exp_t, exp_s, scale_ref, mass_ref, feat_ref, weight_ref, feat_out, w0, w1, w2a, w2b, w3, grad_ref
):
    inverse = factor / jnp.sum(mass_ref[...], axis=0)
    rows, cols = exp_t.shape
    count, block = rows // LANES, cols // STEPS
    row = [column(inverse[i : i + 1, :]) for i in range(count)]
    total = [column(inverse[count + i : count + i + 1, :]) for i in range(count)]
    for k, outs in enumerate(((w0,), (w1,), (w2a, w2b), (w3,))):
        for i in range(count):
            r = slice(i * LANES, (i + 1) * LANES)
            for o in range(0, block, LANES):
                c = slice(k * block + o, k * block + o + LANES)
                target = exp_t[r, c] * scale_ref[k : k + 1, o : o + LANES] * row[i]
                grad_ref[r, c] = (exp_s[r, c] * total[i] - target).astype(bf16)
        at = k * block
        for out in outs:
            size = out.shape[0]
            out[...] = lax.dot_general(
                grad_ref[:, at : at + size],
                feat_ref[...],
                (((0,), (0,)), ((), ())),
                preferred_element_type=f32,
            )
            at += size
    feat_out[...] = jnp.dot(grad_ref[...], weight_ref[...], preferred_element_type=f32)


def pair_kernel(mine, other, out):
    half = other.shape[0]
    out[...] = (mine[:half, :] + other[...]).reshape(out.shape)


def relay_kernel(forward, back, upper, lower, forward_out, back_out):
    half = upper.shape[0]
    forward_out[:half, :] = forward[:half, :] + upper[...]
    forward_out[half:, :] = forward[half:, :]
    back_out[:half, :] = back[:half, :]
    back_out[half:, :] = back[half:, :] + lower[...]


def project(raw, grads):
    values = raw.astype(f32)
    inverse = inverse_norm(values)
    unit_rows = values * inverse
    return (grads - unit_rows * jnp.sum(unit_rows * grads, axis=1, keepdims=True)) * inverse


def row_grad_kernel(raw, parts, out):
    out[...] = project(raw[...], jnp.sum(parts[...], axis=0))


def proto_grad_kernel(raw, mine, before, after, out):
    out[...] = project(raw[...], mine[...] + before[...] + after[...])


def shift(values, axis, step):
    size = lax.axis_size(axis)
    return lax.ppermute(values, axis, [(i, (i + step) % size) for i in range(size)])


def spread(values):
    count = lax.axis_size(ROWS)
    return lax.all_to_all(
        jnp.broadcast_to(values[None], (count,) + values.shape), ROWS, 0, 0, tiled=True
    )


def gather_protos(raw, name, flops):
    before, after = shift(raw, "x", 1), shift(raw, "x", -1)
    half = raw.shape[0] // 2
    upper, lower = call(
        halves_kernel, [jax.ShapeDtypeStruct((half, raw.shape[1]), bf16)] * 2, (before, after), flops, name
    )
    return [raw, before, shift(upper, "x", 1), shift(lower, "x", -1), after]


def share(blocks):
    return [blocks[0]] + [shift(blocks[k], "x", k) for k in range(1, STEPS)]


def share_rows(mine, swapped):
    return spread(mine + shift(swapped, "core", 1))


def body(student_rows, teacher_rows, student_protos, teacher_protos):
    own_rows, width = student_rows.shape
    own_protos = student_protos.shape[0]
    rows = own_rows * lax.axis_size(ROWS) * lax.axis_size("core")
    cols = own_protos * STEPS
    factor = own_protos * 256 / 16.0
    work = 2 * rows * cols * width

    exps = pltpu.VMEM((rows, cols), f32)
    masses = [jax.ShapeDtypeStruct((STEPS, own_protos), f32)] * STEPS
    sums = jax.ShapeDtypeStruct((rows // LANES, LANES), f32)
    feats = pltpu.VMEM((rows, width), bf16)
    weights = pltpu.VMEM((cols, width), bf16)

    peers = lax.axis_size(ROWS)
    packed = call(
        pack_kernel,
        jax.ShapeDtypeStruct((peers, own_rows, 2 * width), bf16),
        [pltpu.with_memory_space_constraint(r, pltpu.HBM) for r in (teacher_rows, student_rows)],
        0,
        "pack",
        [pltpu.VMEM((2, own_rows, width), bf16), pltpu.SemaphoreType.DMA((2,))],
        where=pl.BlockSpec(memory_space=pltpu.HBM),
    )
    own = lax.all_to_all(packed, ROWS, 0, 0, tiled=True).reshape(-1, 2 * width)
    teacher_blocks = gather_protos(teacher_protos, "teacher_halves", 100 * work)
    teacher_weight = call(unit_kernel, weights, teacher_blocks, 0, "teacher_units")
    student_raw, teacher_blocks[1] = lax.optimization_barrier((student_protos, teacher_blocks[1]))
    student_blocks = gather_protos(student_raw, "student_halves", 0)
    own, teacher_weight, student_blocks[1], student_blocks[4] = lax.optimization_barrier(
        (own, teacher_weight, student_blocks[1], student_blocks[4])
    )
    student_weight = call(unit_kernel, weights, student_blocks, 0, "student_units")
    sib = shift(own, "core", 1)

    exp_t, *mass = call(
        teacher_kernel, [exps] + masses + [feats], (own, sib, teacher_weight), work, "teacher"
    )
    mass = share(mass[:STEPS])
    mass[3], student_weight = lax.optimization_barrier((mass[3], student_weight))
    exp_s, student_sums, student_feat = call(
        student_kernel, [exps, sums, feats], (own, sib, student_weight), work, "student"
    )
    for sweep in range(SWEEPS):
        last = sweep + 1 == SWEEPS
        extra = (student_sums,) if last else ()
        out = jax.ShapeDtypeStruct((rows // LANES * (1 + len(extra)), LANES), f32)
        mine, swapped, scale = call(
            row_kernel,
            [out, out, masses[0]],
            (exp_t, *mass, *extra),
            work // 8,
            "rows",
        )
        row_masses = share_rows(mine, swapped)
        if not last:
            mass = share(call(column_kernel, masses, (exp_t, row_masses), work // 8, "columns"))

    feat_grad, *weight_parts = call(
        functools.partial(grads_kernel, factor),
        [
            jax.ShapeDtypeStruct((size, width), f32)
            for size in (rows, own_protos, own_protos, own_protos // 2, own_protos // 2, own_protos)
        ],
        (exp_t, exp_s, scale, row_masses, student_feat, student_weight),
        2 * work,
        "grads",
        [pltpu.VMEM((rows, cols), bf16)],
    )
    half = rows // 2
    feat_pair = call(
        pair_kernel,
        jax.ShapeDtypeStruct((half // own_rows, own_rows, width), f32),
        (feat_grad, shift(feat_grad[half:], "core", 1)),
        100 * work,
        "pair",
    )
    feat_share = lax.all_to_all(feat_pair, ROWS, 0, 0, tiled=True)
    own_part, back_part, upper_part, lower_part, forward_part = weight_parts
    forward_part, back_part = call(
        relay_kernel,
        [jax.ShapeDtypeStruct((own_protos, width), f32)] * 2,
        (forward_part, back_part, shift(upper_part, "x", 1), shift(lower_part, "x", -1)),
        100 * work,
        "relay",
    )
    proto_grad = call(
        proto_grad_kernel,
        jax.ShapeDtypeStruct((own_protos, width), f32),
        (student_protos, own_part, shift(forward_part, "x", 1), shift(back_part, "x", -1)),
        0,
        "proto_grad",
    )
    row_grad = call(
        row_grad_kernel,
        jax.ShapeDtypeStruct((own_rows, width), f32),
        (student_rows, feat_share),
        0,
        "row_grad",
    )
    return (row_grad, proto_grad)


def solution(mesh):
    fine = Mesh(mesh.devices.reshape(4, 4, 8, 2), ("y", "x", "z", "core"))
    rows = P(("y", "x", "z", "core"), None)
    protos = P(("z", "core", "y", "x"), None)
    return jax.shard_map(
        body,
        mesh=fine,
        in_specs=(rows, rows, protos, protos),
        out_specs=(rows, protos),
        check_vma=False,
    )
```

```python
import functools

import jax
import jax.numpy as jnp
from jax import lax
from jax.experimental import pallas as pl
from jax.experimental.pallas import tpu as pltpu
from jax.sharding import Mesh, PartitionSpec as P

SWEEPS = 3
TEACHER_TEMP = 0.04
STUDENT_TEMP = 0.1
EPSILON = 1e-06
ROWS = ("y", "z")
STEPS = 4
LANES = 128
TILE = 256

f32 = jnp.float32
bf16 = jnp.bfloat16
VMEM = pl.BlockSpec(memory_space=pltpu.VMEM)


def inverse_norm(values):
    return lax.rsqrt(jnp.sum(values * values, axis=1, keepdims=True) + EPSILON)


def unit(raw):
    values = raw.astype(f32)
    return (values * inverse_norm(values)).astype(bf16)


def call(kernel, outs, operands, flops, name, scratch=(), after=(), where=VMEM):
    count = len(after)
    return pl.pallas_call(
        lambda *refs: kernel(*refs[count:]),
        out_shape=outs,
        in_specs=[pl.BlockSpec(memory_space=pl.ANY)] * count + [where] * len(operands),
        out_specs=jax.tree.map(lambda unused: VMEM, outs),
        scratch_shapes=scratch,
        compiler_params=pltpu.CompilerParams(vmem_limit_bytes=8 * 2**20),
        cost_estimate=pl.CostEstimate(flops=flops, bytes_accessed=2**20, transcendentals=0),
        name=name,
    )(*after, *operands)


def column(values):
    return jnp.broadcast_to(values, (LANES, LANES)).T


def row_of_sums(block):
    return jnp.sum(block.T, axis=0, keepdims=True)


def lane_sum(values):
    total = values[:, :LANES]
    for at in range(LANES, values.shape[1], LANES):
        total = total + values[:, at : at + LANES]
    return total


def store_rolled(outs, block, values):
    for step, out in enumerate(outs):
        at = (block + step) % STEPS
        out[at : at + 1, :] = values


def pack_kernel(first, second, out, held, arrived):
    copies = [
        pltpu.make_async_copy(ref, held.at[k], arrived.at[k]) for k, ref in enumerate((first, second))
    ]
    for copy in copies:
        copy.start()
    for copy in copies:
        copy.wait()
    packed = jnp.concatenate([held[0], held[1]], axis=1)
    for peer in range(out.shape[0]):
        out[peer] = packed


def halves_kernel(before, after, upper, lower):
    half = upper.shape[0]
    upper[...] = before[:half, :]
    lower[...] = after[half:, :]


def unit_kernel(*refs):
    out, at = refs[-1], 0
    for ref in refs[:-1]:
        out[at : at + ref.shape[0], :] = unit(ref[...])
        at += ref.shape[0]


def load_features(first, own, sib, feat_ref):
    half, width = own.shape[0], feat_ref.shape[1]
    feat_ref[:half, :] = unit(own[:, first : first + width])
    feat_ref[half:, :] = unit(sib[:, first : first + width])


def scores(rows, weights):
    return lax.dot_general(rows, weights, (((1,), (1,)), ((), ())), preferred_element_type=f32)


def teacher_kernel(own, sib, weight_ref, exp_ref, m0, m1, m2, m3, feat_ref):
    load_features(0, own, sib, feat_ref)
    rows, block = feat_ref.shape[0], weight_ref.shape[0] // STEPS
    for k in range(STEPS):
        cols = slice(k * block, (k + 1) * block)
        total = jnp.zeros((8, block), f32)
        for at in range(0, rows, TILE):
            r = slice(at, at + TILE)
            part = jnp.exp(scores(feat_ref[r, :], weight_ref[cols, :]) * (1.0 / TEACHER_TEMP))
            exp_ref[r, cols] = part
            total = total + jnp.sum(part.reshape(TILE // 8, 8, block), axis=0)
        store_rolled((m0, m1, m2, m3), k, jnp.sum(total, axis=0, keepdims=True))


def student_kernel(own, sib, weight_ref, exp_ref, sum_ref, feat_ref):
    load_features(feat_ref.shape[1], own, sib, feat_ref)
    rows, block = feat_ref.shape[0], weight_ref.shape[0] // STEPS
    for at in range(0, rows, TILE):
        r = slice(at, at + TILE)
        total = jnp.zeros((TILE, LANES), f32)
        for k in range(STEPS):
            cols = slice(k * block, (k + 1) * block)
            part = jnp.exp(scores(feat_ref[r, :], weight_ref[cols, :]) * (1.0 / STUDENT_TEMP))
            exp_ref[r, cols] = part
            total = total + lane_sum(part)
        for t in range(TILE // LANES):
            i = at // LANES + t
            sum_ref[i : i + 1, :] = row_of_sums(total[t * LANES : (t + 1) * LANES])


def column_kernel(exp_ref, mass_ref, m0, m1, m2, m3):
    scale = 1.0 / jnp.sum(mass_ref[...], axis=0)
    rows, cols = exp_ref.shape
    block = cols // STEPS
    wide = 2 * block
    for h in range(cols // wide):
        total = jnp.zeros((8, wide), f32)
        for i in range(rows // LANES):
            col = column(scale[i : i + 1, :])
            for j in range(0, LANES, 8):
                at = i * LANES + j
                factor = jnp.concatenate([col[j : j + 8, :]] * (wide // LANES), axis=1)
                total = total + exp_ref[at : at + 8, h * wide : (h + 1) * wide] * factor
        whole = jnp.sum(total, axis=0, keepdims=True)
        for b in range(2):
            store_rolled((m0, m1, m2, m3), 2 * h + b, whole[:, b * block : (b + 1) * block])


def row_kernel(exp_ref, m0, m1, m2, m3, *refs):
    extra, (out_ref, swap_ref, scale_ref) = refs[:-3], refs[-3:]
    scale = 1.0 / (m0[...] + m1[...] + m2[...] + m3[...])
    scale_ref[...] = scale
    rows, cols = exp_ref.shape
    block = cols // STEPS
    count = rows // LANES
    for i in range(count):
        total = jnp.zeros((LANES, LANES), f32)
        for at in range(0, cols, LANES):
            k, o = at // block, at % block
            r = slice(i * LANES, (i + 1) * LANES)
            total = total + exp_ref[r, at : at + LANES] * scale[k : k + 1, o : o + LANES]
        out_ref[i : i + 1, :] = row_of_sums(total)
    half = count // 2
    swap_ref[:half, :] = out_ref[half:, :]
    swap_ref[half:, :] = out_ref[:half, :]
    for ref in extra:
        out_ref[half:, :] = ref[:half, :]
        swap_ref[half:, :] = ref[half:, :]


def scale_kernel(factor, mass_ref, out_ref):
    out_ref[...] = factor / jnp.sum(mass_ref[...], axis=0)


def logits_kernel(first, exp_t, exp_s, scale_ref, inverse_ref, weight_ref, grad_ref, feat_out):
    rows, cols = grad_ref.shape
    count, block = rows // LANES, cols // STEPS
    for i in range(count):
        r = slice(i * LANES, (i + 1) * LANES)
        e = slice(first + i * LANES, first + (i + 1) * LANES)
        row = column(inverse_ref[i : i + 1, :])
        total = column(inverse_ref[count + i : count + i + 1, :])
        for at in range(0, cols, LANES):
            k, o = at // block, at % block
            c = slice(at, at + LANES)
            target = exp_t[e, c] * scale_ref[k : k + 1, o : o + LANES] * row
            grad_ref[r, c] = (exp_s[e, c] * total - target).astype(bf16)
    feat_out[...] = jnp.dot(grad_ref[...], weight_ref[...], preferred_element_type=f32)


def weights_kernel(grad_own, grad_sib, feat_ref, *outs):
    half = grad_own.shape[0]
    at = 0
    for out in outs:
        size = out.shape[0]
        total = 0.0
        for grad_ref, first in ((grad_own, 0), (grad_sib, half)):
            total = total + lax.dot_general(
                grad_ref[:, at : at + size],
                feat_ref[first : first + half, :],
                (((0,), (0,)), ((), ())),
                preferred_element_type=f32,
            )
        out[...] = total
        at += size


def pair_kernel(mine, other, out):
    out[...] = (mine[...] + other[...]).reshape(out.shape)


def relay_kernel(forward, back, upper, lower, forward_out, back_out):
    half = upper.shape[0]
    forward_out[:half, :] = forward[:half, :] + upper[...]
    forward_out[half:, :] = forward[half:, :]
    back_out[:half, :] = back[:half, :]
    back_out[half:, :] = back[half:, :] + lower[...]


def project(raw, grads):
    values = raw.astype(f32)
    inverse = inverse_norm(values)
    unit_rows = values * inverse
    return (grads - unit_rows * jnp.sum(unit_rows * grads, axis=1, keepdims=True)) * inverse


def row_grad_kernel(raw, parts, out):
    out[...] = project(raw[...], jnp.sum(parts[...], axis=0))


def proto_grad_kernel(raw, mine, before, after, out):
    out[...] = project(raw[...], mine[...] + before[...] + after[...])


def shift(values, axis, step):
    size = lax.axis_size(axis)
    return lax.ppermute(values, axis, [(i, (i + step) % size) for i in range(size)])


def spread(values):
    count = lax.axis_size(ROWS)
    return lax.all_to_all(
        jnp.broadcast_to(values[None], (count,) + values.shape), ROWS, 0, 0, tiled=True
    )


def gather_protos(raw, name, flops):
    before, after = shift(raw, "x", 1), shift(raw, "x", -1)
    half = raw.shape[0] // 2
    upper, lower = call(
        halves_kernel, [jax.ShapeDtypeStruct((half, raw.shape[1]), bf16)] * 2, (before, after), flops, name
    )
    return [raw, before, shift(upper, "x", 1), shift(lower, "x", -1), after]


def share(blocks):
    return [blocks[0]] + [shift(blocks[k], "x", k) for k in range(1, STEPS)]


def share_rows(mine, swapped):
    return spread(mine + shift(swapped, "core", 1))


def body(student_rows, teacher_rows, student_protos, teacher_protos):
    own_rows, width = student_rows.shape
    own_protos = student_protos.shape[0]
    rows = own_rows * lax.axis_size(ROWS) * lax.axis_size("core")
    cols = own_protos * STEPS
    factor = own_protos * 256 / 16.0
    work = 2 * rows * cols * width

    exps = pltpu.VMEM((rows, cols), f32)
    masses = [jax.ShapeDtypeStruct((STEPS, own_protos), f32)] * STEPS
    sums = jax.ShapeDtypeStruct((rows // LANES, LANES), f32)
    feats = pltpu.VMEM((rows, width), bf16)
    weights = pltpu.VMEM((cols, width), bf16)

    peers = lax.axis_size(ROWS)
    packed = call(
        pack_kernel,
        jax.ShapeDtypeStruct((peers, own_rows, 2 * width), bf16),
        [pltpu.with_memory_space_constraint(r, pltpu.HBM) for r in (teacher_rows, student_rows)],
        0,
        "pack",
        [pltpu.VMEM((2, own_rows, width), bf16), pltpu.SemaphoreType.DMA((2,))],
        where=pl.BlockSpec(memory_space=pltpu.HBM),
    )
    own = lax.all_to_all(packed, ROWS, 0, 0, tiled=True).reshape(-1, 2 * width)
    teacher_blocks = gather_protos(teacher_protos, "teacher_halves", 100 * work)
    teacher_weight = call(unit_kernel, weights, teacher_blocks, 0, "teacher_units")
    student_raw, teacher_blocks[1] = lax.optimization_barrier((student_protos, teacher_blocks[1]))
    student_blocks = gather_protos(student_raw, "student_halves", 0)
    own, teacher_weight, student_blocks[1], student_blocks[4] = lax.optimization_barrier(
        (own, teacher_weight, student_blocks[1], student_blocks[4])
    )
    student_weight = call(unit_kernel, weights, student_blocks, 0, "student_units")
    sib = shift(own, "core", 1)

    exp_t, *mass = call(
        teacher_kernel, [exps] + masses + [feats], (own, sib, teacher_weight), work, "teacher"
    )
    mass = share(mass[:STEPS])
    mass[3], student_weight = lax.optimization_barrier((mass[3], student_weight))
    exp_s, student_sums, student_feat = call(
        student_kernel, [exps, sums, feats], (own, sib, student_weight), work, "student"
    )
    for sweep in range(SWEEPS):
        last = sweep + 1 == SWEEPS
        extra = (student_sums,) if last else ()
        out = jax.ShapeDtypeStruct((rows // LANES, LANES), f32)
        mine, swapped, scale = call(
            row_kernel,
            [out, out, masses[0]],
            (exp_t, *mass, *extra),
            work // 8,
            "rows",
        )
        row_masses = share_rows(mine, swapped)
        if not last:
            mass = share(call(column_kernel, masses, (exp_t, row_masses), work // 8, "columns"))

    half = rows // 2
    inverse = call(
        functools.partial(scale_kernel, factor),
        jax.ShapeDtypeStruct((rows // LANES, LANES), f32),
        (row_masses,),
        0,
        "scales",
    )
    def logits(first, scales, after):
        return call(
            functools.partial(logits_kernel, first),
            [pltpu.VMEM((half, cols), bf16), jax.ShapeDtypeStruct((half, width), f32)],
            (exp_t, exp_s, scale, scales, student_weight),
            work // 2,
            "logits",
            after=after,
        )

    own_grads, own_feat = logits(0, inverse, ())
    sib_grads, sib_feat = logits(half, shift(inverse, "core", 1), (own_feat,))
    weight_parts = call(
        weights_kernel,
        [
            jax.ShapeDtypeStruct((size, width), f32)
            for size in (own_protos, own_protos, own_protos // 2, own_protos // 2, own_protos)
        ],
        (own_grads, sib_grads, student_feat),
        work,
        "weights",
    )
    feat_pair = call(
        pair_kernel,
        jax.ShapeDtypeStruct((half // own_rows, own_rows, width), f32),
        (own_feat, shift(sib_feat, "core", 1)),
        100 * work,
        "pair",
        after=weight_parts[:1],
    )
    feat_share = lax.all_to_all(feat_pair, ROWS, 0, 0, tiled=True)
    own_part, back_part, upper_part, lower_part, forward_part = weight_parts
    forward_part, back_part = call(
        relay_kernel,
        [jax.ShapeDtypeStruct((own_protos, width), f32)] * 2,
        (forward_part, back_part, shift(upper_part, "x", 1), shift(lower_part, "x", -1)),
        100 * work,
        "relay",
    )
    proto_grad = call(
        proto_grad_kernel,
        jax.ShapeDtypeStruct((own_protos, width), f32),
        (student_protos, own_part, shift(forward_part, "x", 1), shift(back_part, "x", -1)),
        0,
        "proto_grad",
    )
    row_grad = call(
        row_grad_kernel,
        jax.ShapeDtypeStruct((own_rows, width), f32),
        (student_rows, feat_share),
        0,
        "row_grad",
    )
    return (row_grad, proto_grad)


def solution(mesh):
    fine = Mesh(mesh.devices.reshape(4, 4, 8, 2), ("y", "x", "z", "core"))
    rows = P(("y", "x", "z", "core"), None)
    protos = P(("z", "core", "y", "x"), None)
    return jax.shard_map(
        body,
        mesh=fine,
        in_specs=(rows, rows, protos, protos),
        out_specs=(rows, protos),
        check_vma=False,
    )
```

```python
import functools

import jax
import jax.numpy as jnp
from jax import lax
from jax.experimental import pallas as pl
from jax.experimental.pallas import tpu as pltpu
from jax.sharding import Mesh, PartitionSpec as P

SWEEPS = 3
TEACHER_TEMP = 0.04
STUDENT_TEMP = 0.1
EPSILON = 1e-06
ROWS = ("y", "z")
STEPS = 4
LANES = 128
TILE = 256

f32 = jnp.float32
bf16 = jnp.bfloat16
VMEM = pl.BlockSpec(memory_space=pltpu.VMEM)


def inverse_norm(values):
    return lax.rsqrt(jnp.sum(values * values, axis=1, keepdims=True) + EPSILON)


def unit(raw):
    values = raw.astype(f32)
    return (values * inverse_norm(values)).astype(bf16)


def call(kernel, outs, operands, flops, name, scratch=(), after=(), where=VMEM):
    count = len(after)
    return pl.pallas_call(
        lambda *refs: kernel(*refs[count:]),
        out_shape=outs,
        in_specs=[pl.BlockSpec(memory_space=pl.ANY)] * count + [where] * len(operands),
        out_specs=jax.tree.map(lambda unused: VMEM, outs),
        scratch_shapes=scratch,
        compiler_params=pltpu.CompilerParams(vmem_limit_bytes=8 * 2**20),
        cost_estimate=pl.CostEstimate(flops=flops, bytes_accessed=2**20, transcendentals=0),
        name=name,
    )(*after, *operands)


def column(values):
    return jnp.broadcast_to(values, (LANES, LANES)).T


def row_of_sums(block):
    return jnp.sum(block.T, axis=0, keepdims=True)


def lane_sum(values):
    total = values[:, :LANES]
    for at in range(LANES, values.shape[1], LANES):
        total = total + values[:, at : at + LANES]
    return total


def store_rolled(outs, block, values):
    for step, out in enumerate(outs):
        at = (block + step) % STEPS
        out[at : at + 1, :] = values


def pack_kernel(first, second, out, held, arrived):
    copies = [
        pltpu.make_async_copy(ref, held.at[k], arrived.at[k]) for k, ref in enumerate((first, second))
    ]
    for copy in copies:
        copy.start()
    for copy in copies:
        copy.wait()
    packed = jnp.concatenate([held[0], held[1]], axis=1)
    for peer in range(out.shape[0]):
        out[peer] = packed


def halves_kernel(before, after, upper, lower):
    half = upper.shape[0]
    upper[...] = before[:half, :]
    lower[...] = after[half:, :]


def unit_kernel(*refs):
    out, at = refs[-1], 0
    for ref in refs[:-1]:
        out[at : at + ref.shape[0], :] = unit(ref[...])
        at += ref.shape[0]


def load_features(first, own, sib, feat_ref):
    half, width = own.shape[0], feat_ref.shape[1]
    feat_ref[:half, :] = unit(own[:, first : first + width])
    feat_ref[half:, :] = unit(sib[:, first : first + width])


def scores(rows, weights):
    return lax.dot_general(rows, weights, (((1,), (1,)), ((), ())), preferred_element_type=f32)


def teacher_masses(raw, weight_ref, exp_ref, feat_ref, before):
    feat_ref[...] = unit(raw[:, : feat_ref.shape[1]])
    rows, block = feat_ref.shape[0], weight_ref.shape[0] // STEPS
    for k in range(STEPS):
        cols = slice(k * block, (k + 1) * block)
        total = before(k)
        for at in range(0, rows, TILE):
            r = slice(at, at + TILE)
            part = jnp.exp(scores(feat_ref[r, :], weight_ref[cols, :]) * (1.0 / TEACHER_TEMP))
            exp_ref[r, cols] = part
            total = total + jnp.sum(part.reshape(TILE // 8, 8, block), axis=0)
        yield k, cols, total


def teacher_own_kernel(own, weight_ref, exp_ref, mass_ref, feat_ref):
    zero = jnp.zeros((8, weight_ref.shape[0] // STEPS), f32)
    for k, cols, total in teacher_masses(own, weight_ref, exp_ref, feat_ref, lambda unused: zero):
        mass_ref[:, cols] = total


def teacher_sib_kernel(sib, weight_ref, mass_ref, exp_ref, m0, m1, m2, m3, feat_ref):
    block = weight_ref.shape[0] // STEPS

    def before(k):
        return mass_ref[:, k * block : (k + 1) * block]

    for k, cols, total in teacher_masses(sib, weight_ref, exp_ref, feat_ref, before):
        store_rolled((m0, m1, m2, m3), k, jnp.sum(total, axis=0, keepdims=True))


def student_kernel(own, sib, weight_ref, exp_ref, sum_ref, feat_ref):
    load_features(feat_ref.shape[1], own, sib, feat_ref)
    rows, block = feat_ref.shape[0], weight_ref.shape[0] // STEPS
    for at in range(0, rows, TILE):
        r = slice(at, at + TILE)
        total = jnp.zeros((TILE, LANES), f32)
        for k in range(STEPS):
            cols = slice(k * block, (k + 1) * block)
            part = jnp.exp(scores(feat_ref[r, :], weight_ref[cols, :]) * (1.0 / STUDENT_TEMP))
            exp_ref[r, cols] = part
            total = total + lane_sum(part)
        for t in range(TILE // LANES):
            i = at // LANES + t
            sum_ref[i : i + 1, :] = row_of_sums(total[t * LANES : (t + 1) * LANES])


def column_kernel(exp_own, exp_sib, mass_ref, m0, m1, m2, m3):
    scale = 1.0 / jnp.sum(mass_ref[...], axis=0)
    rows, cols = exp_own.shape
    block = cols // STEPS
    wide = 2 * block
    for h in range(cols // wide):
        total = jnp.zeros((8, wide), f32)
        for i in range(2 * rows // LANES):
            exp_ref, first = (exp_own, exp_sib)[i * LANES // rows], i * LANES % rows
            col = column(scale[i : i + 1, :])
            for j in range(0, LANES, 8):
                factor = jnp.concatenate([col[j : j + 8, :]] * (wide // LANES), axis=1)
                at = first + j
                total = total + exp_ref[at : at + 8, h * wide : (h + 1) * wide] * factor
        whole = jnp.sum(total, axis=0, keepdims=True)
        for b in range(2):
            store_rolled((m0, m1, m2, m3), 2 * h + b, whole[:, b * block : (b + 1) * block])


def row_kernel(exp_own, exp_sib, m0, m1, m2, m3, *refs):
    extra, (out_ref, swap_ref, scale_ref) = refs[:-3], refs[-3:]
    scale = 1.0 / (m0[...] + m1[...] + m2[...] + m3[...])
    scale_ref[...] = scale
    rows, cols = exp_own.shape
    block = cols // STEPS
    half = rows // LANES
    for i in range(2 * half):
        exp_ref, first = (exp_own, exp_sib)[i // half], i % half * LANES
        total = jnp.zeros((LANES, LANES), f32)
        for at in range(0, cols, LANES):
            k, o = at // block, at % block
            r = slice(first, first + LANES)
            total = total + exp_ref[r, at : at + LANES] * scale[k : k + 1, o : o + LANES]
        out_ref[i : i + 1, :] = row_of_sums(total)
    swap_ref[:half, :] = out_ref[half:, :]
    swap_ref[half:, :] = out_ref[:half, :]
    for ref in extra:
        out_ref[half:, :] = ref[:half, :]
        swap_ref[half:, :] = ref[half:, :]


def scale_kernel(factor, mass_ref, out_ref):
    out_ref[...] = factor / jnp.sum(mass_ref[...], axis=0)


def logits_kernel(first, exp_t, exp_s, scale_ref, inverse_ref, weight_ref, grad_ref, feat_out):
    rows, cols = grad_ref.shape
    count, block = rows // LANES, cols // STEPS
    for i in range(count):
        r = slice(i * LANES, (i + 1) * LANES)
        e = slice(first + i * LANES, first + (i + 1) * LANES)
        row = column(inverse_ref[i : i + 1, :])
        total = column(inverse_ref[count + i : count + i + 1, :])
        for at in range(0, cols, LANES):
            k, o = at // block, at % block
            c = slice(at, at + LANES)
            target = exp_t[r, c] * scale_ref[k : k + 1, o : o + LANES] * row
            grad_ref[r, c] = (exp_s[e, c] * total - target).astype(bf16)
    feat_out[...] = jnp.dot(grad_ref[...], weight_ref[...], preferred_element_type=f32)


def weights_kernel(
    grad_own, grad_sib, feat_ref, mine, forward, back, forward_last, back_last
):
    half = mine.shape[0] // 2
    few = forward.shape[0] - half
    whole = slice(0, half)
    places = (
        ((mine, 0, whole),),
        ((mine, half, whole),),
        ((back, half, slice(0, few)), (back_last, half, slice(few, half))),
        ((back_last, 0, whole),),
        ((forward, 0, whole),),
        ((back, 0, whole),),
        ((forward_last, 0, whole),),
        ((forward, half, slice(0, few)), (forward_last, half, slice(few, half))),
    )
    rows = grad_own.shape[0]
    for k, stores in enumerate(places):
        total = 0.0
        for grad_ref, first in ((grad_own, 0), (grad_sib, rows)):
            total = total + lax.dot_general(
                grad_ref[:, k * half : (k + 1) * half],
                feat_ref[first : first + rows, :],
                (((0,), (0,)), ((), ())),
                preferred_element_type=f32,
            )
        for out, at, taken in stores:
            part = total[taken]
            out[at : at + part.shape[0], :] = part


def pair_kernel(mine, other, out):
    out[...] = (mine[...] + other[...]).reshape(out.shape)


def relay_kernel(forward, back, before, after, forward_out, back_out):
    half = (forward.shape[0] + before.shape[0]) // 3
    for mine, got, out in ((forward, before, forward_out), (back, after, back_out)):
        out[:half, :] = mine[:half, :] + got[:half, :]
        out[half:, :] = mine[half:, :]


def project(raw, grads):
    values = raw.astype(f32)
    inverse = inverse_norm(values)
    unit_rows = values * inverse
    return (grads - unit_rows * jnp.sum(unit_rows * grads, axis=1, keepdims=True)) * inverse


def row_grad_kernel(raw, parts, out):
    out[...] = project(raw[...], jnp.sum(parts[...], axis=0))


def proto_grad_kernel(raw, mine, before, after, before_last, after_last, out):
    half = out.shape[0] // 2
    few = before.shape[0] - half
    places = (
        (0, few, before_last, 0, after, half),
        (few, half - few, before_last, few, after_last, half),
        (half, few, after_last, 0, before, half),
        (half + few, half - few, after_last, few, before_last, half),
    )
    for at, size, one, i, two, j in places:
        r = slice(at, at + size)
        sums = mine[r, :] + one[i : i + size, :] + two[j : j + size, :]
        out[r, :] = project(raw[r, :], sums)


def shift(values, axis, step):
    size = lax.axis_size(axis)
    return lax.ppermute(values, axis, [(i, (i + step) % size) for i in range(size)])


def spread(values):
    count = lax.axis_size(ROWS)
    return lax.all_to_all(
        jnp.broadcast_to(values[None], (count,) + values.shape), ROWS, 0, 0, tiled=True
    )


def gather_protos(raw, name, flops):
    before, after = shift(raw, "x", 1), shift(raw, "x", -1)
    half = raw.shape[0] // 2
    upper, lower = call(
        halves_kernel, [jax.ShapeDtypeStruct((half, raw.shape[1]), bf16)] * 2, (before, after), flops, name
    )
    return [raw, before, shift(upper, "x", 1), shift(lower, "x", -1), after]


def share(blocks):
    return [blocks[0]] + [shift(blocks[k], "x", k) for k in (2, 3, 1)]


def body(student_rows, teacher_rows, student_protos, teacher_protos):
    own_rows, width = student_rows.shape
    own_protos = student_protos.shape[0]
    rows = own_rows * lax.axis_size(ROWS) * lax.axis_size("core")
    cols = own_protos * STEPS
    factor = own_protos * 256 / 16.0
    work = 2 * rows * cols * width

    exps = pltpu.VMEM((rows, cols), f32)
    masses = [jax.ShapeDtypeStruct((STEPS, own_protos), f32)] * STEPS
    sums = jax.ShapeDtypeStruct((rows // LANES, LANES), f32)
    feats = pltpu.VMEM((rows, width), bf16)
    weights = pltpu.VMEM((cols, width), bf16)

    peers = lax.axis_size(ROWS)
    packed = call(
        pack_kernel,
        jax.ShapeDtypeStruct((peers, own_rows, 2 * width), bf16),
        [pltpu.with_memory_space_constraint(r, pltpu.HBM) for r in (teacher_rows, student_rows)],
        0,
        "pack",
        [pltpu.VMEM((2, own_rows, width), bf16), pltpu.SemaphoreType.DMA((2,))],
        where=pl.BlockSpec(memory_space=pltpu.HBM),
    )
    own = lax.all_to_all(packed, ROWS, 0, 0, tiled=True).reshape(-1, 2 * width)
    teacher_blocks = gather_protos(teacher_protos, "teacher_halves", 100 * work)
    teacher_weight = call(unit_kernel, weights, teacher_blocks, 0, "teacher_units")
    student_raw, teacher_blocks[1] = lax.optimization_barrier((student_protos, teacher_blocks[1]))
    student_blocks = gather_protos(student_raw, "student_halves", 0)
    own, teacher_weight, student_blocks[1], student_blocks[4] = lax.optimization_barrier(
        (own, teacher_weight, student_blocks[1], student_blocks[4])
    )
    student_weight = call(unit_kernel, weights, student_blocks, 0, "student_units")
    sib = shift(own, "core", 1)

    half = rows // 2
    half_exps, half_feats = pltpu.VMEM((half, cols), f32), [pltpu.VMEM((half, width), bf16)]
    exp_own, mass = call(
        teacher_own_kernel,
        [half_exps, jax.ShapeDtypeStruct((8, cols), f32)],
        (own, teacher_weight),
        work // 2,
        "teacher_own",
        half_feats,
    )
    exp_sib, *mass = call(
        teacher_sib_kernel,
        [half_exps] + masses,
        (sib, teacher_weight, mass),
        work // 2,
        "teacher_sib",
        half_feats,
    )
    mass = share(mass)
    for sweep in range(SWEEPS):
        last = sweep + 1 == SWEEPS
        extra = (student_sums,) if last else ()
        out = jax.ShapeDtypeStruct((rows // LANES, LANES), f32)
        mine, swapped, scale = call(
            row_kernel,
            [out, out, masses[0]],
            (exp_own, exp_sib, *mass, *extra),
            work // 8,
            "rows",
        )
        row_masses = mine + shift(swapped, "core", 1)
        if sweep == 0:
            row_masses, student_weight = lax.optimization_barrier((row_masses, student_weight))
            exp_s, student_sums, student_feat = call(
                student_kernel, [exps, sums, feats], (own, sib, student_weight), work, "student"
            )
        row_masses = spread(row_masses)
        if not last:
            mass = share(call(column_kernel, masses, (exp_own, exp_sib, row_masses), work // 8, "columns"))

    inverse = call(
        functools.partial(scale_kernel, factor),
        jax.ShapeDtypeStruct((rows // LANES, LANES), f32),
        (row_masses,),
        0,
        "scales",
    )
    def logits(first, exp_t, scales, after):
        return call(
            functools.partial(logits_kernel, first),
            [pltpu.VMEM((half, cols), bf16), jax.ShapeDtypeStruct((half, width), f32)],
            (exp_t, exp_s, scale, scales, student_weight),
            work // 2,
            "logits",
            after=after,
        )

    own_grads, own_feat = logits(0, exp_own, inverse, ())
    sib_grads, sib_feat = logits(half, exp_sib, shift(inverse, "core", 1), (own_feat,))
    pre, post = own_protos * 5 // 8, own_protos * (12 - 5) // 8
    weight_parts = call(
        weights_kernel,
        [
            jax.ShapeDtypeStruct((size, width), f32)
            for size in (own_protos, pre, pre, post, post)
        ],
        (own_grads, sib_grads, student_feat),
        work,
        "weights",
    )
    feat_pair = call(
        pair_kernel,
        jax.ShapeDtypeStruct((half // own_rows, own_rows, width), f32),
        (own_feat, shift(sib_feat, "core", 1)),
        100 * work,
        "pair",
        after=weight_parts[:1],
    )
    feat_share = lax.all_to_all(feat_pair, ROWS, 0, 0, tiled=True)
    own_part, forward_part, back_part, forward_last, back_last = weight_parts
    before, after = shift(forward_part, "x", 1), shift(back_part, "x", -1)
    forward_last, back_last = call(
        relay_kernel,
        [jax.ShapeDtypeStruct(forward_last.shape, f32)] * 2,
        (forward_last, back_last, before, after),
        100 * work,
        "relay",
    )
    last = (shift(forward_last, "x", 1), shift(back_last, "x", -1))
    proto_grad = call(
        proto_grad_kernel,
        jax.ShapeDtypeStruct((own_protos, width), f32),
        (student_protos, own_part, before, after, *last),
        0,
        "proto_grad",
    )
    row_grad = call(
        row_grad_kernel,
        jax.ShapeDtypeStruct((own_rows, width), f32),
        (student_rows, feat_share),
        0,
        "row_grad",
    )
    return (row_grad, proto_grad)


def solution(mesh):
    fine = Mesh(mesh.devices.reshape(4, 4, 8, 2), ("y", "x", "z", "core"))
    rows = P(("y", "x", "z", "core"), None)
    protos = P(("z", "core", "y", "x"), None)
    return jax.shard_map(
        body,
        mesh=fine,
        in_specs=(rows, rows, protos, protos),
        out_specs=(rows, protos),
        check_vma=False,
    )
```

```python
import functools

import jax
import jax.numpy as jnp
from jax import lax
from jax.experimental import pallas as pl
from jax.experimental.pallas import tpu as pltpu
from jax.sharding import Mesh, PartitionSpec as P

SWEEPS = 3
TEACHER_TEMP = 0.04
STUDENT_TEMP = 0.1
EPSILON = 1e-06
ROWS = ("y", "z")
STEPS = 4
LANES = 128
TILE = 256

f32 = jnp.float32
bf16 = jnp.bfloat16
VMEM = pl.BlockSpec(memory_space=pltpu.VMEM)


def inverse_norm(values):
    return lax.rsqrt(jnp.sum(values * values, axis=1, keepdims=True) + EPSILON)


def unit(raw):
    values = raw.astype(f32)
    return (values * inverse_norm(values)).astype(bf16)


def call(kernel, outs, operands, flops, name, scratch=(), after=(), where=VMEM):
    count = len(after)
    return pl.pallas_call(
        lambda *refs: kernel(*refs[count:]),
        out_shape=outs,
        in_specs=[pl.BlockSpec(memory_space=pl.ANY)] * count + [where] * len(operands),
        out_specs=jax.tree.map(lambda unused: VMEM, outs),
        scratch_shapes=scratch,
        compiler_params=pltpu.CompilerParams(vmem_limit_bytes=8 * 2**20),
        cost_estimate=pl.CostEstimate(flops=flops, bytes_accessed=2**20, transcendentals=0),
        name=name,
    )(*after, *operands)


def column(values):
    return jnp.broadcast_to(values, (LANES, LANES)).T


def row_of_sums(block):
    return jnp.sum(block.T, axis=0, keepdims=True)


def lane_sum(values):
    total = values[:, :LANES]
    for at in range(LANES, values.shape[1], LANES):
        total = total + values[:, at : at + LANES]
    return total


def store_rolled(outs, block, values):
    for step, out in enumerate(outs):
        at = (block + step) % STEPS
        out[at : at + 1, :] = values


def pack_kernel(first, second, out, held, arrived):
    copies = [
        pltpu.make_async_copy(ref, held.at[k], arrived.at[k]) for k, ref in enumerate((first, second))
    ]
    for copy in copies:
        copy.start()
    for copy in copies:
        copy.wait()
    packed = jnp.concatenate([held[0], held[1]], axis=1)
    for peer in range(out.shape[0]):
        out[peer] = packed


def halves_kernel(before, after, upper, lower):
    half = upper.shape[0]
    upper[...] = before[:half, :]
    lower[...] = after[half:, :]


def unit_kernel(*refs):
    out, at = refs[-1], 0
    for ref in refs[:-1]:
        out[at : at + ref.shape[0], :] = unit(ref[...])
        at += ref.shape[0]


def load_features(first, own, sib, feat_ref):
    half, width = own.shape[0], feat_ref.shape[1]
    feat_ref[:half, :] = unit(own[:, first : first + width])
    feat_ref[half:, :] = unit(sib[:, first : first + width])


def scores(rows, weights):
    return lax.dot_general(rows, weights, (((1,), (1,)), ((), ())), preferred_element_type=f32)


def teacher_masses(raw, weight_ref, exp_ref, feat_ref, before):
    feat_ref[...] = unit(raw[:, : feat_ref.shape[1]])
    rows, block = feat_ref.shape[0], weight_ref.shape[0] // STEPS
    for k in range(STEPS):
        cols = slice(k * block, (k + 1) * block)
        total = before(k)
        for at in range(0, rows, TILE):
            r = slice(at, at + TILE)
            part = jnp.exp(scores(feat_ref[r, :], weight_ref[cols, :]) * (1.0 / TEACHER_TEMP))
            exp_ref[r, cols] = part
            total = total + jnp.sum(part.reshape(TILE // 8, 8, block), axis=0)
        yield k, cols, total


def teacher_own_kernel(own, weight_ref, exp_ref, mass_ref, feat_ref):
    zero = jnp.zeros((8, weight_ref.shape[0] // STEPS), f32)
    for k, cols, total in teacher_masses(own, weight_ref, exp_ref, feat_ref, lambda unused: zero):
        mass_ref[:, cols] = total


def teacher_sib_kernel(sib, weight_ref, mass_ref, exp_ref, m0, m1, m2, m3, feat_ref):
    block = weight_ref.shape[0] // STEPS

    def before(k):
        return mass_ref[:, k * block : (k + 1) * block]

    for k, cols, total in teacher_masses(sib, weight_ref, exp_ref, feat_ref, before):
        store_rolled((m0, m1, m2, m3), k, jnp.sum(total, axis=0, keepdims=True))


def student_kernel(own, sib, weight_ref, exp_ref, sum_ref, feat_ref):
    load_features(feat_ref.shape[1], own, sib, feat_ref)
    rows, block = feat_ref.shape[0], weight_ref.shape[0] // STEPS
    for at in range(0, rows, TILE):
        r = slice(at, at + TILE)
        total = jnp.zeros((TILE, LANES), f32)
        for k in range(STEPS):
            cols = slice(k * block, (k + 1) * block)
            part = jnp.exp(scores(feat_ref[r, :], weight_ref[cols, :]) * (1.0 / STUDENT_TEMP))
            exp_ref[r, cols] = part
            total = total + lane_sum(part)
        for t in range(TILE // LANES):
            i = at // LANES + t
            sum_ref[i : i + 1, :] = row_of_sums(total[t * LANES : (t + 1) * LANES])


def column_kernel(exp_own, exp_sib, mass_ref, m0, m1, m2, m3):
    scale = 1.0 / jnp.sum(mass_ref[...], axis=0)
    rows, cols = exp_own.shape
    block = cols // STEPS
    wide = 2 * block
    for h in range(cols // wide):
        total = jnp.zeros((8, wide), f32)
        for i in range(2 * rows // LANES):
            exp_ref, first = (exp_own, exp_sib)[i * LANES // rows], i * LANES % rows
            col = column(scale[i : i + 1, :])
            for j in range(0, LANES, 8):
                factor = jnp.concatenate([col[j : j + 8, :]] * (wide // LANES), axis=1)
                at = first + j
                total = total + exp_ref[at : at + 8, h * wide : (h + 1) * wide] * factor
        whole = jnp.sum(total, axis=0, keepdims=True)
        for b in range(2):
            store_rolled((m0, m1, m2, m3), 2 * h + b, whole[:, b * block : (b + 1) * block])


def row_kernel(exp_own, exp_sib, m0, m1, m2, m3, *refs):
    extra, (out_ref, swap_ref, scale_ref) = refs[:-3], refs[-3:]
    scale = 1.0 / (m0[...] + m1[...] + m2[...] + m3[...])
    scale_ref[...] = scale
    rows, cols = exp_own.shape
    block = cols // STEPS
    half = rows // LANES
    for i in range(2 * half):
        exp_ref, first = (exp_own, exp_sib)[i // half], i % half * LANES
        total = jnp.zeros((LANES, LANES), f32)
        for at in range(0, cols, LANES):
            k, o = at // block, at % block
            r = slice(first, first + LANES)
            total = total + exp_ref[r, at : at + LANES] * scale[k : k + 1, o : o + LANES]
        out_ref[i : i + 1, :] = row_of_sums(total)
    swap_ref[:half, :] = out_ref[half:, :]
    swap_ref[half:, :] = out_ref[:half, :]
    for ref in extra:
        out_ref[half:, :] = ref[:half, :]
        swap_ref[half:, :] = ref[half:, :]


def scale_kernel(factor, mass_ref, out_ref):
    out_ref[...] = factor / jnp.sum(mass_ref[...], axis=0)


def logits_kernel(first, exp_t, exp_s, scale_ref, inverse_ref, weight_ref, grad_ref, feat_out):
    rows, cols = grad_ref.shape
    count, block = rows // LANES, cols // STEPS
    for i in range(count):
        r = slice(i * LANES, (i + 1) * LANES)
        e = slice(first + i * LANES, first + (i + 1) * LANES)
        row = column(inverse_ref[i : i + 1, :])
        total = column(inverse_ref[count + i : count + i + 1, :])
        for at in range(0, cols, LANES):
            k, o = at // block, at % block
            c = slice(at, at + LANES)
            target = exp_t[r, c] * scale_ref[k : k + 1, o : o + LANES] * row
            grad_ref[r, c] = (exp_s[e, c] * total - target).astype(bf16)
    feat_out[...] = jnp.dot(grad_ref[...], weight_ref[...], preferred_element_type=f32)


def weights_kernel(
    grad_own, grad_sib, feat_ref, mine, forward, back, forward_last, back_last
):
    half = mine.shape[0] // 2
    few = forward.shape[0] - half
    whole = slice(0, half)
    places = (
        ((mine, 0, whole),),
        ((mine, half, whole),),
        ((back, half, slice(0, few)), (back_last, half, slice(few, half))),
        ((back_last, 0, whole),),
        ((forward, 0, whole),),
        ((back, 0, whole),),
        ((forward_last, 0, whole),),
        ((forward, half, slice(0, few)), (forward_last, half, slice(few, half))),
    )
    rows = grad_own.shape[0]
    for k, stores in enumerate(places):
        total = 0.0
        for grad_ref, first in ((grad_own, 0), (grad_sib, rows)):
            total = total + lax.dot_general(
                grad_ref[:, k * half : (k + 1) * half],
                feat_ref[first : first + rows, :],
                (((0,), (0,)), ((), ())),
                preferred_element_type=f32,
            )
        for out, at, taken in stores:
            part = total[taken]
            out[at : at + part.shape[0], :] = part


def pair_kernel(mine, other, out):
    out[...] = (mine[...] + other[...]).reshape(out.shape)


def relay_kernel(forward, back, before, after, forward_out, back_out):
    half = (forward.shape[0] + before.shape[0]) // 3
    for mine, got, out in ((forward, before, forward_out), (back, after, back_out)):
        out[:half, :] = mine[:half, :] + got[:half, :]
        out[half:, :] = mine[half:, :]


def project(raw, grads):
    values = raw.astype(f32)
    inverse = inverse_norm(values)
    unit_rows = values * inverse
    return (grads - unit_rows * jnp.sum(unit_rows * grads, axis=1, keepdims=True)) * inverse


def row_grad_kernel(raw, parts, out):
    out[...] = project(raw[...], jnp.sum(parts[...], axis=0))


def proto_grad_kernel(raw, mine, before, after, before_last, after_last, out):
    half = out.shape[0] // 2
    few = before.shape[0] - half
    places = (
        (0, few, before_last, 0, after, half),
        (few, half - few, before_last, few, after_last, half),
        (half, few, after_last, 0, before, half),
        (half + few, half - few, after_last, few, before_last, half),
    )
    for at, size, one, i, two, j in places:
        r = slice(at, at + size)
        sums = mine[r, :] + one[i : i + size, :] + two[j : j + size, :]
        out[r, :] = project(raw[r, :], sums)


def shift(values, axis, step):
    size = lax.axis_size(axis)
    return lax.ppermute(values, axis, [(i, (i + step) % size) for i in range(size)])


def spread(values):
    count = lax.axis_size(ROWS)
    return lax.all_to_all(
        jnp.broadcast_to(values[None], (count,) + values.shape), ROWS, 0, 0, tiled=True
    )


def gather_protos(raw, name, flops):
    before, after = shift(raw, "x", 1), shift(raw, "x", -1)
    half = raw.shape[0] // 2
    upper, lower = call(
        halves_kernel, [jax.ShapeDtypeStruct((half, raw.shape[1]), bf16)] * 2, (before, after), flops, name
    )
    return [raw, before, shift(upper, "x", 1), shift(lower, "x", -1), after]


def share(blocks):
    return [blocks[0]] + [shift(blocks[k], "x", k) for k in (2, 3, 1)]


def body(student_rows, teacher_rows, student_protos, teacher_protos):
    own_rows, width = student_rows.shape
    own_protos = student_protos.shape[0]
    rows = own_rows * lax.axis_size(ROWS) * lax.axis_size("core")
    cols = own_protos * STEPS
    factor = own_protos * 256 / 16.0
    work = 2 * rows * cols * width

    exps = pltpu.VMEM((rows, cols), f32)
    masses = [jax.ShapeDtypeStruct((STEPS, own_protos), f32)] * STEPS
    sums = jax.ShapeDtypeStruct((rows // LANES, LANES), f32)
    feats = pltpu.VMEM((rows, width), bf16)
    weights = pltpu.VMEM((cols, width), bf16)

    peers = lax.axis_size(ROWS)
    packed = call(
        pack_kernel,
        jax.ShapeDtypeStruct((peers, own_rows, 2 * width), bf16),
        [pltpu.with_memory_space_constraint(r, pltpu.HBM) for r in (teacher_rows, student_rows)],
        0,
        "pack",
        [pltpu.VMEM((2, own_rows, width), bf16), pltpu.SemaphoreType.DMA((2,))],
        where=pl.BlockSpec(memory_space=pltpu.HBM),
    )
    own = lax.all_to_all(packed, ROWS, 0, 0, tiled=True).reshape(-1, 2 * width)
    teacher_blocks = gather_protos(teacher_protos, "teacher_halves", 100 * work)
    teacher_weight = call(unit_kernel, weights, teacher_blocks, 0, "teacher_units")
    student_raw, teacher_blocks[1] = lax.optimization_barrier((student_protos, teacher_blocks[1]))
    student_blocks = gather_protos(student_raw, "student_halves", 0)
    own, teacher_weight, student_blocks[1], student_blocks[4] = lax.optimization_barrier(
        (own, teacher_weight, student_blocks[1], student_blocks[4])
    )
    student_weight = call(unit_kernel, weights, student_blocks, 0, "student_units")
    sib = shift(own, "core", 1)

    half = rows // 2
    half_exps, half_feats = pltpu.VMEM((half, cols), f32), [pltpu.VMEM((half, width), bf16)]
    exp_own, mass = call(
        teacher_own_kernel,
        [half_exps, jax.ShapeDtypeStruct((8, cols), f32)],
        (own, teacher_weight),
        work // 2,
        "teacher_own",
        half_feats,
    )
    exp_sib, *mass = call(
        teacher_sib_kernel,
        [half_exps] + masses,
        (sib, teacher_weight, mass),
        work // 2,
        "teacher_sib",
        half_feats,
    )
    mass = share(mass)
    for sweep in range(SWEEPS):
        last = sweep + 1 == SWEEPS
        extra = (student_sums,) if last else ()
        out = jax.ShapeDtypeStruct((rows // LANES, LANES), f32)
        mine, swapped, scale = call(
            row_kernel,
            [out, out, masses[0]],
            (exp_own, exp_sib, *mass, *extra),
            work // 8,
            "rows",
        )
        row_masses = mine + shift(swapped, "core", 1)
        if sweep == 0:
            row_masses, student_weight = lax.optimization_barrier((row_masses, student_weight))
            exp_s, student_sums, student_feat = call(
                student_kernel, [exps, sums, feats], (own, sib, student_weight), work, "student"
            )
        row_masses = spread(row_masses)
        if not last:
            mass = share(call(column_kernel, masses, (exp_own, exp_sib, row_masses), work // 8, "columns"))
        if sweep == 0:
            mass[3], student_sums = lax.optimization_barrier((mass[3], student_sums))

    inverse = call(
        functools.partial(scale_kernel, factor),
        jax.ShapeDtypeStruct((rows // LANES, LANES), f32),
        (row_masses,),
        0,
        "scales",
    )
    def logits(first, exp_t, scales, after):
        return call(
            functools.partial(logits_kernel, first),
            [pltpu.VMEM((half, cols), bf16), jax.ShapeDtypeStruct((half, width), f32)],
            (exp_t, exp_s, scale, scales, student_weight),
            work // 2,
            "logits",
            after=after,
        )

    own_grads, own_feat = logits(0, exp_own, inverse, ())
    sib_grads, sib_feat = logits(half, exp_sib, shift(inverse, "core", 1), (own_feat,))
    pre, post = own_protos * 5 // 8, own_protos * (12 - 5) // 8
    weight_parts = call(
        weights_kernel,
        [
            jax.ShapeDtypeStruct((size, width), f32)
            for size in (own_protos, pre, pre, post, post)
        ],
        (own_grads, sib_grads, student_feat),
        work,
        "weights",
    )
    feat_pair = call(
        pair_kernel,
        jax.ShapeDtypeStruct((half // own_rows, own_rows, width), f32),
        (own_feat, shift(sib_feat, "core", 1)),
        100 * work,
        "pair",
        after=weight_parts[:1],
    )
    feat_share = lax.all_to_all(feat_pair, ROWS, 0, 0, tiled=True)
    own_part, forward_part, back_part, forward_last, back_last = weight_parts
    before, after = shift(forward_part, "x", 1), shift(back_part, "x", -1)
    forward_last, back_last = call(
        relay_kernel,
        [jax.ShapeDtypeStruct(forward_last.shape, f32)] * 2,
        (forward_last, back_last, before, after),
        100 * work,
        "relay",
    )
    last = (shift(forward_last, "x", 1), shift(back_last, "x", -1))
    proto_grad = call(
        proto_grad_kernel,
        jax.ShapeDtypeStruct((own_protos, width), f32),
        (student_protos, own_part, before, after, *last),
        0,
        "proto_grad",
    )
    row_grad = call(
        row_grad_kernel,
        jax.ShapeDtypeStruct((own_rows, width), f32),
        (student_rows, feat_share),
        0,
        "row_grad",
    )
    return (row_grad, proto_grad)


def solution(mesh):
    fine = Mesh(mesh.devices.reshape(4, 4, 8, 2), ("y", "x", "z", "core"))
    rows = P(("y", "x", "z", "core"), None)
    protos = P(("z", "core", "y", "x"), None)
    return jax.shard_map(
        body,
        mesh=fine,
        in_specs=(rows, rows, protos, protos),
        out_specs=(rows, protos),
        check_vma=False,
    )
```

```python
import functools

import jax
import jax.numpy as jnp
from jax import lax
from jax.experimental import pallas as pl
from jax.experimental.pallas import tpu as pltpu
from jax.sharding import Mesh, PartitionSpec as P

SWEEPS = 3
TEACHER_TEMP = 0.04
STUDENT_TEMP = 0.1
EPSILON = 1e-06
ROWS = ("y", "z")
STEPS = 4
LANES = 128
TILE = 256

f32 = jnp.float32
bf16 = jnp.bfloat16
VMEM = pl.BlockSpec(memory_space=pltpu.VMEM)


def inverse_norm(values):
    return lax.rsqrt(jnp.sum(values * values, axis=1, keepdims=True) + EPSILON)


def unit(raw):
    values = raw.astype(f32)
    return (values * inverse_norm(values)).astype(bf16)


def call(kernel, outs, operands, flops, name, scratch=(), after=(), where=VMEM):
    count = len(after)
    return pl.pallas_call(
        lambda *refs: kernel(*refs[count:]),
        out_shape=outs,
        in_specs=[pl.BlockSpec(memory_space=pl.ANY)] * count + [where] * len(operands),
        out_specs=jax.tree.map(lambda unused: VMEM, outs),
        scratch_shapes=scratch,
        compiler_params=pltpu.CompilerParams(vmem_limit_bytes=8 * 2**20),
        cost_estimate=pl.CostEstimate(flops=flops, bytes_accessed=2**20, transcendentals=0),
        name=name,
    )(*after, *operands)


def column(values):
    return jnp.broadcast_to(values, (LANES, LANES)).T


def row_of_sums(block):
    return jnp.sum(block.T, axis=0, keepdims=True)


def lane_sum(values):
    total = values[:, :LANES]
    for at in range(LANES, values.shape[1], LANES):
        total = total + values[:, at : at + LANES]
    return total


def store_rolled(outs, block, values):
    for step, out in enumerate(outs):
        at = (block + step) % STEPS
        out[at : at + 1, :] = values


def pack_kernel(first, second, out, held, arrived):
    copies = [
        pltpu.make_async_copy(ref, held.at[k], arrived.at[k]) for k, ref in enumerate((first, second))
    ]
    for copy in copies:
        copy.start()
    for copy in copies:
        copy.wait()
    packed = jnp.concatenate([held[0], held[1]], axis=1)
    for peer in range(out.shape[0]):
        out[peer] = packed


def halves_kernel(before, after, upper, lower):
    half = upper.shape[0]
    upper[...] = before[:half, :]
    lower[...] = after[half:, :]


def unit_kernel(*refs):
    out, at = refs[-1], 0
    for ref in refs[:-1]:
        out[at : at + ref.shape[0], :] = unit(ref[...])
        at += ref.shape[0]


def load_features(first, own, sib, feat_ref):
    half, width = own.shape[0], feat_ref.shape[1]
    feat_ref[:half, :] = unit(own[:, first : first + width])
    feat_ref[half:, :] = unit(sib[:, first : first + width])


def scores(rows, weights):
    return lax.dot_general(rows, weights, (((1,), (1,)), ((), ())), preferred_element_type=f32)


def teacher_masses(raw, weight_ref, exp_ref, feat_ref, before):
    feat_ref[...] = unit(raw[:, : feat_ref.shape[1]])
    rows, block = feat_ref.shape[0], weight_ref.shape[0] // STEPS
    for k in range(STEPS):
        cols = slice(k * block, (k + 1) * block)
        total = before(k)
        for at in range(0, rows, TILE):
            r = slice(at, at + TILE)
            part = jnp.exp(scores(feat_ref[r, :], weight_ref[cols, :]) * (1.0 / TEACHER_TEMP))
            exp_ref[r, cols] = part
            total = total + jnp.sum(part.reshape(TILE // 8, 8, block), axis=0)
        yield k, cols, total


def teacher_own_kernel(own, weight_ref, exp_ref, mass_ref, feat_ref):
    zero = jnp.zeros((8, weight_ref.shape[0] // STEPS), f32)
    for k, cols, total in teacher_masses(own, weight_ref, exp_ref, feat_ref, lambda unused: zero):
        mass_ref[:, cols] = total


def teacher_sib_kernel(sib, weight_ref, mass_ref, exp_ref, m0, m1, m2, m3, feat_ref):
    block = weight_ref.shape[0] // STEPS

    def before(k):
        return mass_ref[:, k * block : (k + 1) * block]

    for k, cols, total in teacher_masses(sib, weight_ref, exp_ref, feat_ref, before):
        store_rolled((m0, m1, m2, m3), k, jnp.sum(total, axis=0, keepdims=True))


def student_kernel(own, sib, weight_ref, exp_ref, sum_ref, feat_ref):
    load_features(feat_ref.shape[1], own, sib, feat_ref)
    rows, block = feat_ref.shape[0], weight_ref.shape[0] // STEPS
    for at in range(0, rows, TILE):
        r = slice(at, at + TILE)
        total = jnp.zeros((TILE, LANES), f32)
        for k in range(STEPS):
            cols = slice(k * block, (k + 1) * block)
            part = jnp.exp(scores(feat_ref[r, :], weight_ref[cols, :]) * (1.0 / STUDENT_TEMP))
            exp_ref[r, cols] = part
            total = total + lane_sum(part)
        for t in range(TILE // LANES):
            i = at // LANES + t
            sum_ref[i : i + 1, :] = row_of_sums(total[t * LANES : (t + 1) * LANES])


def column_kernel(exp_own, exp_sib, mass_ref, m0, m1, m2, m3):
    scale = 1.0 / jnp.sum(mass_ref[...], axis=0)
    rows, cols = exp_own.shape
    block = cols // STEPS
    wide = 2 * block
    for h in range(cols // wide):
        total = jnp.zeros((8, wide), f32)
        for i in range(2 * rows // LANES):
            exp_ref, first = (exp_own, exp_sib)[i * LANES // rows], i * LANES % rows
            col = column(scale[i : i + 1, :])
            for j in range(0, LANES, 8):
                factor = jnp.concatenate([col[j : j + 8, :]] * (wide // LANES), axis=1)
                at = first + j
                total = total + exp_ref[at : at + 8, h * wide : (h + 1) * wide] * factor
        whole = jnp.sum(total, axis=0, keepdims=True)
        for b in range(2):
            store_rolled((m0, m1, m2, m3), 2 * h + b, whole[:, b * block : (b + 1) * block])


def row_kernel(exp_own, exp_sib, m0, m1, m2, m3, *refs):
    extra, (out_ref, swap_ref, scale_ref) = refs[:-3], refs[-3:]
    scale = 1.0 / (m0[...] + m1[...] + m2[...] + m3[...])
    scale_ref[...] = scale
    rows, cols = exp_own.shape
    block = cols // STEPS
    half = rows // LANES
    for i in range(2 * half):
        exp_ref, first = (exp_own, exp_sib)[i // half], i % half * LANES
        total = jnp.zeros((LANES, LANES), f32)
        for at in range(0, cols, LANES):
            k, o = at // block, at % block
            r = slice(first, first + LANES)
            total = total + exp_ref[r, at : at + LANES] * scale[k : k + 1, o : o + LANES]
        out_ref[i : i + 1, :] = row_of_sums(total)
    swap_ref[:half, :] = out_ref[half:, :]
    swap_ref[half:, :] = out_ref[:half, :]
    for ref in extra:
        out_ref[half:, :] = ref[:half, :]
        swap_ref[half:, :] = ref[half:, :]


def scale_kernel(factor, mass_ref, out_ref):
    out_ref[...] = factor / jnp.sum(mass_ref[...], axis=0)


def logits_kernel(first, exp_t, exp_s, scale_ref, inverse_ref, weight_ref, grad_ref, feat_out):
    rows, cols = grad_ref.shape
    count, block = rows // LANES, cols // STEPS
    for i in range(count):
        r = slice(i * LANES, (i + 1) * LANES)
        e = slice(first + i * LANES, first + (i + 1) * LANES)
        row = column(inverse_ref[i : i + 1, :])
        total = column(inverse_ref[count + i : count + i + 1, :])
        for at in range(0, cols, LANES):
            k, o = at // block, at % block
            c = slice(at, at + LANES)
            target = exp_t[r, c] * scale_ref[k : k + 1, o : o + LANES] * row
            grad_ref[r, c] = (exp_s[e, c] * total - target).astype(bf16)
    feat_out[...] = jnp.dot(grad_ref[...], weight_ref[...], preferred_element_type=f32)


def weights_kernel(
    grad_own, grad_sib, feat_ref, mine, forward, back, forward_last, back_last
):
    half = mine.shape[0] // 2
    few = forward.shape[0] - half
    whole = slice(0, half)
    places = (
        ((mine, 0, whole),),
        ((mine, half, whole),),
        ((back, half, slice(0, few)), (back_last, half, slice(few, half))),
        ((back_last, 0, whole),),
        ((forward, 0, whole),),
        ((back, 0, whole),),
        ((forward_last, 0, whole),),
        ((forward, half, slice(0, few)), (forward_last, half, slice(few, half))),
    )
    rows = grad_own.shape[0]
    for k, stores in enumerate(places):
        total = 0.0
        for grad_ref, first in ((grad_own, 0), (grad_sib, rows)):
            total = total + lax.dot_general(
                grad_ref[:, k * half : (k + 1) * half],
                feat_ref[first : first + rows, :],
                (((0,), (0,)), ((), ())),
                preferred_element_type=f32,
            )
        for out, at, taken in stores:
            part = total[taken]
            out[at : at + part.shape[0], :] = part


def pair_kernel(mine, other, out):
    out[...] = (mine[...] + other[...]).reshape(out.shape)


def relay_kernel(forward, back, before, after, forward_out, back_out):
    half = (forward.shape[0] + before.shape[0]) // 3
    for mine, got, out in ((forward, before, forward_out), (back, after, back_out)):
        out[:half, :] = mine[:half, :] + got[:half, :]
        out[half:, :] = mine[half:, :]


def project(raw, grads):
    values = raw.astype(f32)
    inverse = inverse_norm(values)
    unit_rows = values * inverse
    return (grads - unit_rows * jnp.sum(unit_rows * grads, axis=1, keepdims=True)) * inverse


def row_grad_kernel(raw, parts, out):
    out[...] = project(raw[...], jnp.sum(parts[...], axis=0))


def proto_grad_kernel(raw, mine, before, after, before_last, after_last, out):
    half = out.shape[0] // 2
    few = before.shape[0] - half
    places = (
        (0, few, before_last, 0, after, half),
        (few, half - few, before_last, few, after_last, half),
        (half, few, after_last, 0, before, half),
        (half + few, half - few, after_last, few, before_last, half),
    )
    for at, size, one, i, two, j in places:
        r = slice(at, at + size)
        sums = mine[r, :] + one[i : i + size, :] + two[j : j + size, :]
        out[r, :] = project(raw[r, :], sums)


def shift(values, axis, step):
    size = lax.axis_size(axis)
    return lax.ppermute(values, axis, [(i, (i + step) % size) for i in range(size)])


def spread(values):
    count = lax.axis_size(ROWS)
    return lax.all_to_all(
        jnp.broadcast_to(values[None], (count,) + values.shape), ROWS, 0, 0, tiled=True
    )


def gather_protos(raw, name, flops):
    before, after = shift(raw, "x", 1), shift(raw, "x", -1)
    half = raw.shape[0] // 2
    upper, lower = call(
        halves_kernel, [jax.ShapeDtypeStruct((half, raw.shape[1]), bf16)] * 2, (before, after), flops, name
    )
    return [raw, before, shift(upper, "x", 1), shift(lower, "x", -1), after]


def share(blocks):
    return [blocks[0]] + [shift(blocks[k], "x", k) for k in (2, 3, 1)]


def body(student_rows, teacher_rows, student_protos, teacher_protos):
    own_rows, width = student_rows.shape
    own_protos = student_protos.shape[0]
    rows = own_rows * lax.axis_size(ROWS) * lax.axis_size("core")
    cols = own_protos * STEPS
    factor = own_protos * 256 / 16.0
    work = 2 * rows * cols * width

    exps = pltpu.VMEM((rows, cols), f32)
    masses = [jax.ShapeDtypeStruct((STEPS, own_protos), f32)] * STEPS
    sums = jax.ShapeDtypeStruct((rows // LANES, LANES), f32)
    feats = pltpu.VMEM((rows, width), bf16)
    weights = pltpu.VMEM((cols, width), bf16)

    peers = lax.axis_size(ROWS)
    packed = call(
        pack_kernel,
        jax.ShapeDtypeStruct((peers, own_rows, 2 * width), bf16),
        [pltpu.with_memory_space_constraint(r, pltpu.HBM) for r in (teacher_rows, student_rows)],
        0,
        "pack",
        [pltpu.VMEM((2, own_rows, width), bf16), pltpu.SemaphoreType.DMA((2,))],
        where=pl.BlockSpec(memory_space=pltpu.HBM),
    )
    own = lax.all_to_all(packed, ROWS, 0, 0, tiled=True).reshape(-1, 2 * width)
    teacher_blocks = gather_protos(teacher_protos, "teacher_halves", 100 * work)
    teacher_weight = call(unit_kernel, weights, teacher_blocks, 0, "teacher_units")
    student_raw, teacher_blocks[1] = lax.optimization_barrier((student_protos, teacher_blocks[1]))
    student_blocks = gather_protos(student_raw, "student_halves", 0)
    own, teacher_weight, student_blocks[1], student_blocks[4] = lax.optimization_barrier(
        (own, teacher_weight, student_blocks[1], student_blocks[4])
    )
    student_weight = call(unit_kernel, weights, student_blocks, 0, "student_units")
    sib = shift(own, "core", 1)

    half = rows // 2
    half_exps, half_feats = pltpu.VMEM((half, cols), f32), [pltpu.VMEM((half, width), bf16)]
    exp_own, mass = call(
        teacher_own_kernel,
        [half_exps, jax.ShapeDtypeStruct((8, cols), f32)],
        (own, teacher_weight),
        work // 2,
        "teacher_own",
        half_feats,
    )
    exp_sib, *mass = call(
        teacher_sib_kernel,
        [half_exps] + masses,
        (sib, teacher_weight, mass),
        work // 2,
        "teacher_sib",
        half_feats,
    )
    mass = share(mass)
    for sweep in range(SWEEPS):
        last = sweep + 1 == SWEEPS
        extra = (student_sums,) if last else ()
        out = jax.ShapeDtypeStruct((rows // LANES, LANES), f32)
        mine, swapped, scale = call(
            row_kernel,
            [out, out, masses[0]],
            (exp_own, exp_sib, *mass, *extra),
            work // 8,
            "rows",
        )
        row_masses = mine + shift(swapped, "core", 1)
        if sweep == 0:
            row_masses, student_weight = lax.optimization_barrier((row_masses, student_weight))
            exp_s, student_sums, student_feat = call(
                student_kernel, [exps, sums, feats], (own, sib, student_weight), work, "student"
            )
        row_masses = spread(row_masses)
        if not last:
            mass = share(call(column_kernel, masses, (exp_own, exp_sib, row_masses), work // 8, "columns"))
        if sweep == 0:
            mass[3], student_sums = lax.optimization_barrier((mass[3], student_sums))

    inverse = call(
        functools.partial(scale_kernel, factor),
        jax.ShapeDtypeStruct((rows // LANES, LANES), f32),
        (row_masses,),
        0,
        "scales",
    )
    def logits(first, exp_t, scales, after):
        return call(
            functools.partial(logits_kernel, first),
            [pltpu.VMEM((half, cols), bf16), jax.ShapeDtypeStruct((half, width), f32)],
            (exp_t, exp_s, scale, scales, student_weight),
            work // 2,
            "logits",
            after=after,
        )

    own_grads, own_feat = logits(0, exp_own, inverse, ())
    sib_grads, sib_feat = logits(half, exp_sib, shift(inverse, "core", 1), (own_feat,))
    pre, post = own_protos * 11 // 16, own_protos * 13 // 16
    weight_parts = call(
        weights_kernel,
        [
            jax.ShapeDtypeStruct((size, width), f32)
            for size in (own_protos, pre, pre, post, post)
        ],
        (own_grads, sib_grads, student_feat),
        work,
        "weights",
    )
    feat_pair = call(
        pair_kernel,
        jax.ShapeDtypeStruct((half // own_rows, own_rows, width), f32),
        (own_feat, shift(sib_feat, "core", 1)),
        100 * work,
        "pair",
        after=weight_parts[:1],
    )
    feat_share = lax.all_to_all(feat_pair, ROWS, 0, 0, tiled=True)
    own_part, forward_part, back_part, forward_last, back_last = weight_parts
    before, after = shift(forward_part, "x", 1), shift(back_part, "x", -1)
    forward_last, back_last = call(
        relay_kernel,
        [jax.ShapeDtypeStruct(forward_last.shape, f32)] * 2,
        (forward_last, back_last, before, after),
        100 * work,
        "relay",
    )
    last = (shift(forward_last, "x", 1), shift(back_last, "x", -1))
    proto_grad = call(
        proto_grad_kernel,
        jax.ShapeDtypeStruct((own_protos, width), f32),
        (student_protos, own_part, before, after, *last),
        0,
        "proto_grad",
    )
    row_grad = call(
        row_grad_kernel,
        jax.ShapeDtypeStruct((own_rows, width), f32),
        (student_rows, feat_share),
        0,
        "row_grad",
    )
    return (row_grad, proto_grad)


def solution(mesh):
    fine = Mesh(mesh.devices.reshape(4, 4, 8, 2), ("y", "x", "z", "core"))
    rows = P(("y", "x", "z", "core"), None)
    protos = P(("z", "core", "y", "x"), None)
    return jax.shard_map(
        body,
        mesh=fine,
        in_specs=(rows, rows, protos, protos),
        out_specs=(rows, protos),
        check_vma=False,
    )
```
